32 devices in a mesh: dp: 8 (over y, x, core), mp: 4 (over z).
Axes of the slice: x: 2, y: 2, z: 4, core: 2. Of those that a mesh axis runs over, the one named last changes fastest.
Arguments:
- inputs: bfloat16 [11040, 768], P(('dp', 'mp')), may hold values from -6 to 6
- crop_labels: int32 [11040], P('dp'), may hold values from 0 to 9, as said below
- norm1_gain: bfloat16 [768], replicated, may hold values from 0.5 to 1.5
- norm1_bias: bfloat16 [768], replicated, may hold values from -3 to 3
- qkv_weight: bfloat16 [3, 768, 768], P(None, None, 'mp'), may hold values from -0.3125 to 0.3125
- qv_bias: bfloat16 [2, 768], P(None, 'mp'), may hold values from -3 to 3
- out_weight: bfloat16 [768, 768], P('mp'), may hold values from -1.25 to 1.25
- out_bias: bfloat16 [768], replicated, may hold values from -3 to 3
- norm2_gain: bfloat16 [768], replicated, may hold values from 0.5 to 1.5
- norm2_bias: bfloat16 [768], replicated, may hold values from -3 to 3
- fc1_weight: bfloat16 [768, 3072], P(None, 'mp'), may hold values from -0.21875 to 0.21875
- fc1_bias: bfloat16 [3072], P('mp'), may hold values from -3 to 3
- fc2_weight: bfloat16 [3072, 768], P('mp'), may hold values from -0.109375 to 0.109375
- fc2_bias: bfloat16 [768], replicated, may hold values from -3 to 3
- cotangent: bfloat16 [11040, 768], P(('dp', 'mp')), may hold values from -6 to 6
Outputs:
- layer_out: bfloat16 [11040, 768], P(('dp', 'mp'))
- input_grad: bfloat16 [11040, 768], P(('dp', 'mp'))
- norm1_gain_grad: float32 [768], replicated
- norm1_bias_grad: float32 [768], replicated
- qkv_weight_grad: float32 [3, 768, 768], P(None, None, 'mp')
- qv_bias_grad: float32 [2, 768], P(None, 'mp')
- out_weight_grad: float32 [768, 768], P('mp')
- out_bias_grad: float32 [768], replicated
- norm2_gain_grad: float32 [768], replicated
- norm2_bias_grad: float32 [768], replicated
- fc1_weight_grad: float32 [768, 3072], P(None, 'mp')
- fc1_bias_grad: float32 [3072], P('mp')
- fc2_weight_grad: float32 [3072, 768], P('mp')
- fc2_bias_grad: float32 [768], replicated
The draws below stay inside these ranges and needn't reach their ends.
Inputs may be any that keep to these rules, and one draw needn't show every extreme that they name: `crop_labels`: each aligned run of 690 tokens is one image. Within an image the values 0, 1, 2 and so on each fill one run of consecutive tokens, in increasing order; 2 of these runs have 197 tokens and 8 have 37, in an order drawn for each image.
All inputs are finite; a program needn't handle non-finite values.
Results may differ from the reference program's by a relative error of at most 0.012.
The reference program's roundings to bfloat16 on the way count: a program that leaves them out, or rounds other values in their place, can miss the bound.
Values may be sent and summed in bfloat16 or wider, within the bound.
No kernel may reach another device: no remote copies, remote signals or barrier semaphores. Data moves between devices by JAX's collectives and lax.ppermute only.
A program may use at most 128 MiB of HBM per device.

```python
from functools import partial
import jax
import jax.numpy as jnp
from jax import lax

D = 768
HEADS = 12
HEAD_DIM = 64
FF = 3072
BIG_LEN = 197
SMALL_LEN = 37
BIG_CROPS = 2
SMALL_CROPS = 8
IMG_TOK = 690
IMAGES = 16
TOKENS = 11040


def draw_crop_labels(key, part):
    crop_count = BIG_CROPS + SMALL_CROPS
    image_keys = jax.random.split(key, IMAGES)
    orders = jax.vmap(lambda single: jax.random.permutation(single, crop_count))(image_keys)
    lengths = jnp.where(orders < BIG_CROPS, BIG_LEN, SMALL_LEN).astype(jnp.int32)
    crop_ends = jnp.cumsum(lengths, axis=1).astype(jnp.int32)
    places = jnp.arange(IMG_TOK, dtype=jnp.int32)
    labels = jnp.sum((places[None, :, None] >= crop_ends[:, None, :]).astype(jnp.int32), axis=2)
    return labels.reshape(IMAGES * IMG_TOK).astype(jnp.int32)


def steps_of(stream_key, dims, shards, least, high):
    loudness, own = 1.0, jax.random.fold_in(stream_key, 6)
    for position, parts in shards:
        heights = jnp.exp(jax.random.uniform(jax.random.fold_in(own, position), (parts,), jnp.float32, least / len(shards), high / len(shards)))
        loudness = loudness * jnp.repeat(heights, dims[position] // parts).reshape([-1 if axis == position else 1 for axis in range(len(dims))])
    return loudness


def normal_values(own_key, shape, width, reach, cuts=(), kind=jnp.bfloat16):
    array = jax.random.normal(own_key, shape, jnp.float32) * width
    if len(cuts) > 0:
        array = steps_of(own_key, shape, cuts, -0.22, 0.18) * array
    return jnp.clip(array, min=-reach, max=reach).astype(kind)


def setup_inputs(seed: int = 0) -> dict:
    arg_keys = jax.random.split(jax.random.key(seed), 16)
    return {
        "inputs": normal_values(arg_keys[0], (TOKENS, D), 1.0, 6.0, ((0, 32),)),
        "crop_labels": draw_crop_labels(jax.random.fold_in(arg_keys[15], 71), 0),
        "norm1_gain": jnp.clip(1.0 + 0.1 * jax.random.normal(arg_keys[2], (D,), jnp.float32), 0.5, 1.5).astype(jnp.bfloat16),
        "norm1_bias": normal_values(arg_keys[3], (D,), 0.5, 3.0),
        "qkv_weight": normal_values(arg_keys[4], (3, D, D), (D // 2) ** -0.5, 0.3125, ((2, 4),)),
        "qv_bias": normal_values(arg_keys[5], (2, D), 0.5, 3.0, ((1, 4),)),
        "out_weight": normal_values(arg_keys[6], (D, D), (D // 32) ** -0.5, 1.25, ((0, 4),)),
        "out_bias": normal_values(arg_keys[7], (D,), 0.5, 3.0),
        "norm2_gain": jnp.clip(1.0 + 0.1 * jax.random.normal(arg_keys[8], (D,), jnp.float32), 0.5, 1.5).astype(jnp.bfloat16),
        "norm2_bias": normal_values(arg_keys[9], (D,), 0.5, 3.0),
        "fc1_weight": normal_values(arg_keys[10], (D, FF), D ** -0.5, 0.21875, ((1, 4),)),
        "fc1_bias": normal_values(arg_keys[11], (FF,), 0.5, 3.0, ((0, 4),)),
        "fc2_weight": normal_values(arg_keys[12], (FF, D), FF ** -0.5, 0.109375, ((0, 4),)),
        "fc2_bias": normal_values(arg_keys[13], (D,), 0.5, 3.0),
        "cotangent": normal_values(arg_keys[14], (TOKENS, D), 1.0, 6.0, ((0, 32),)),
    }


@jax.custom_vjp
def low(v):
    return lax.optimization_barrier(v.astype(jnp.bfloat16)).astype(jnp.float32)

@jax.custom_vjp
def low_back(v):
    return v

def low_keep(v):
    return (low(v), None)

def low_pass(kept, grad):
    return (grad,)

def back_keep(v):
    return (v, None)

def back_low(kept, grad):
    return (low(grad),)
low.defvjp(low_keep, low_pass)
low_back.defvjp(back_keep, back_low)
highest = lax.Precision.HIGHEST

def norm_rows(values, norm_gain, norm_shift):
    average = lax.optimization_barrier(jnp.mean(values, axis=-1, keepdims=True))
    centred = values - average
    spread = lax.optimization_barrier(jnp.mean(centred * centred, axis=-1, keepdims=True))
    return centred * lax.rsqrt(spread + 1e-06) * norm_gain + norm_shift

def matmul(left_side, right_side):
    return jnp.dot(left_side, right_side, precision=highest)

def attend_image(packed):
    queries, keys_in, values_in, crop_row = packed
    scores = low_back(jnp.einsum('qhd,khd->hqk', queries, keys_in, precision=highest))
    same_crop = crop_row[:, None] == crop_row[None, :]
    logits = jnp.where(same_crop[None], scores * HEAD_DIM ** (-0.5), -1000000000.0)
    largest = lax.optimization_barrier(jnp.max(logits, axis=-1, keepdims=True))
    exponent = jnp.exp(logits - largest)
    weights = low(exponent / lax.optimization_barrier(jnp.sum(exponent, axis=-1, keepdims=True)))
    return low_back(low(jnp.einsum('hqk,khd->qhd', weights, values_in, precision=highest)))

def layer(crop_labels, inputs, norm1_gain, norm1_bias, qkv_weight, qv_bias, out_weight, out_bias, norm2_gain, norm2_bias, fc1_weight, fc1_bias, fc2_weight, fc2_bias):
    normed = low(norm_rows(inputs, norm1_gain, norm1_bias))
    queries = low_back(low(matmul(normed, qkv_weight[0]) + qv_bias[0]))
    keys_in = low_back(low(matmul(normed, qkv_weight[1])))
    values_in = low_back(low(matmul(normed, qkv_weight[2]) + qv_bias[1]))
    head_shape = (IMAGES, IMG_TOK, HEADS, HEAD_DIM)
    context = lax.map(jax.checkpoint(attend_image), (queries.reshape(head_shape), keys_in.reshape(head_shape), values_in.reshape(head_shape), crop_labels.reshape(IMAGES, IMG_TOK)))
    attended = low_back(matmul(context.reshape(TOKENS, D), out_weight) + out_bias)
    middle = inputs + attended
    normed_two = low(norm_rows(middle, norm2_gain, norm2_bias))
    before = low_back(matmul(normed_two, fc1_weight) + fc1_bias)
    active = low(jax.nn.gelu(before, approximate=False))
    return middle + low_back(matmul(active, fc2_weight) + fc2_bias)

def reference(inputs, crop_labels, norm1_gain, norm1_bias, qkv_weight, qv_bias, out_weight, out_bias, norm2_gain, norm2_bias, fc1_weight, fc1_bias, fc2_weight, fc2_bias, cotangent):
    floats = tuple((array_in.astype(jnp.float32) for array_in in (inputs, norm1_gain, norm1_bias, qkv_weight, qv_bias, out_weight, out_bias, norm2_gain, norm2_bias, fc1_weight, fc1_bias, fc2_weight, fc2_bias)))
    result, pullback = jax.vjp(partial(layer, crop_labels), *floats)
    gradients = pullback(cotangent.astype(jnp.float32))
    return (result.astype(jnp.bfloat16), gradients[0].astype(jnp.bfloat16), gradients[1], gradients[2], gradients[3], gradients[4], gradients[5], gradients[6], gradients[7], gradients[8], gradients[9], gradients[10], gradients[11], gradients[12])
```

```python
import jax
import jax.numpy as jnp
from jax import lax
from jax.experimental import pallas as pl
from jax.experimental.pallas import tpu as pltpu
from jax.sharding import PartitionSpec as P

HEAD_DIM = 64
IMG_TOK = 690
HALF = 345
BIG = 197
SMALL = 37
BIG_PAD = 208
ROWS = 368
D = 768
BF = jnp.bfloat16
F32 = jnp.float32
ALL = ("dp", "mp")


def nt(a, b):
    return lax.dot_general(a, b, (((1,), (1,)), ((), ())), preferred_element_type=F32)


def tn(a, b):
    return lax.dot_general(a, b, (((0,), (0,)), ((), ())), preferred_element_type=F32)


def nn(a, b):
    return lax.dot_general(a, b, (((1,), (0,)), ((), ())), preferred_element_type=F32)


class Routes:
    def __init__(self, dp, mp):
        self.dp, self.mp = dp, mp
        self.groups = dp // 8

        def table(move):
            pairs = []
            for d in range(dp):
                for z in range(mp):
                    g, y, x, c = d >> 3, (d >> 2) & 1, (d >> 1) & 1, d & 1
                    g2, y2, x2, c2, z2 = move(g, y, x, c, z)
                    pairs.append((d * mp + z, (g2 * 8 + y2 * 4 + x2 * 2 + c2) * mp + z2))
            return pairs

        self.core = table(lambda g, y, x, c, z: (g, y, x, 1 - c, z))
        self.first = table(
            lambda g, y, x, c, z: (g, y, 1 - x, c, z) if c == 0 else (g, 1 - y, x, c, z)
        )
        self.second = table(
            lambda g, y, x, c, z: (g, 1 - y, x, c, z) if c == 0 else (g, y, 1 - x, c, z)
        )
        self.x = table(lambda g, y, x, c, z: (g, y, 1 - x, c, z))
        self.y = table(lambda g, y, x, c, z: (g, 1 - y, x, c, z))
        self.z = [table(lambda g, y, x, c, z, k=k: (g, y, x, c, z ^ k)) for k in range(mp)]
        self.image = table(
            lambda g, y, x, c, z: (g, y, x, 1 - c, z ^ 1) if c != (z & 1) else (g, y, x, c, z)
        )
        self.group = [
            table(lambda g, y, x, c, z, b=b: (g ^ b, y, x, c, z))
            for b in (1 << i for i in range(max(self.groups.bit_length() - 1, 0)))
        ]


def send(value, route):
    return lax.ppermute(value, ALL, route)


def choose(stack, places):
    return jnp.stack([lax.dynamic_index_in_dim(stack, i, keepdims=False) for i in places])


def norm_stats(values):
    average = jnp.mean(values, axis=-1, keepdims=True)
    centred = values - average
    spread = jnp.mean(centred * centred, axis=-1, keepdims=True)
    scale = lax.rsqrt(spread + 1e-06)
    return centred * scale, scale


def norm_back(hat, scale, gain, grad):
    inner = grad * gain
    a = jnp.mean(inner, axis=-1, keepdims=True)
    b = jnp.mean(inner * hat, axis=-1, keepdims=True)
    return scale * (inner - a - hat * b)


def block_mask(size, small):
    i = lax.broadcasted_iota(jnp.int32, (size, size), 0)
    j = lax.broadcasted_iota(jnp.int32, (size, size), 1)
    if not small:
        return j < BIG
    return (i // SMALL == j // SMALL) & (j < 4 * SMALL)


def probabilities(q, k, mask):
    logits = jnp.where(mask, nt(q, k) * 0.125, -1e9)
    e = jnp.exp(logits - jnp.max(logits, axis=-1, keepdims=True))
    return e / jnp.sum(e, axis=-1, keepdims=True)


PARTS = ((0, BIG_PAD, False), (BIG_PAD, ROWS - BIG_PAD, True))


def targets(labels, c):
    crops = jnp.arange(10, dtype=jnp.int32)
    member = labels[:, None] == crops[None, :]
    ahead = (crops[None, :] < crops[:, None]).astype(jnp.int32)
    count = jnp.sum(member.astype(jnp.int32), axis=0)
    big = (count > 100).astype(jnp.int32)
    start = jnp.sum(ahead * count[None, :], axis=1)
    rank_big = jnp.sum(ahead * big[None, :], axis=1)
    rank_small = jnp.sum(ahead * (1 - big)[None, :], axis=1)
    core = jnp.where(big == 1, rank_big, rank_small // 4)
    base = jnp.where(big == 1, 0, BIG_PAD + (rank_small % 4) * SMALL)
    shift = jnp.where(core == c, base - start, -100000)
    place = jnp.arange(labels.shape[0], dtype=jnp.int32)
    row = place + jnp.sum(jnp.where(member, shift[None, :], 0), axis=1)
    return jnp.where(row < 0, -1, row)


def kernel(body, outs, args, cost=(1e8, 1e6), scratch=()):
    vmem = pl.BlockSpec(memory_space=pltpu.VMEM)
    smem = pl.BlockSpec(memory_space=pltpu.SMEM)
    return pl.pallas_call(
        body,
        out_shape=tuple(jax.ShapeDtypeStruct(shape, kind) for shape, kind in outs),
        in_specs=[smem if a.ndim == 1 else vmem for a in args],
        out_specs=tuple(vmem for _ in outs),
        scratch_shapes=list(scratch),
        compiler_params=pltpu.CompilerParams(vmem_limit_bytes=40 << 20),
        cost_estimate=pl.CostEstimate(
            flops=int(cost[0]), bytes_accessed=int(cost[1]), transcendentals=0
        ),
    )(*args)


def put_in_order(order, source, out):
    for j in range(8):
        at = pl.multiple_of(order[j] * 96, 96)
        out[96 * j : 96 * j + 96, :] = source[pl.ds(at, 96), :]


def put_back(order, own, oth, out, first=0, size=96):
    for j in range(8):
        at = pl.multiple_of(order[j] * 96, 96)
        part = (own, oth)[j // 4][j % 4, first : first + size, :]
        out[pl.ds(at, size), :] = part.astype(out.dtype)


def select_body(order, xo, xt, go, gt, ro, rt, vec, xs, gs, n1, n1t, gst, flip):
    slots = lax.broadcasted_iota(jnp.int32, (ROWS, HALF), 0)
    pick_own = (slots == ro[...]).astype(F32).astype(BF)
    pick_oth = (slots == rt[...]).astype(F32).astype(BF)
    rows = nn(pick_own, xo[...]) + nn(pick_oth, xt[...])
    xs[...] = rows.astype(BF)
    hat, _ = norm_stats(rows)
    normed = hat * vec[0:1, :] + vec[1:2, :]
    n1[...] = normed.astype(BF)
    flip[...] = normed.astype(BF).T
    put_in_order(order, flip, n1t)
    grads = (nn(pick_own, go[...]) + nn(pick_oth, gt[...])).astype(BF)
    gs[...] = grads
    flip[...] = grads.T
    put_in_order(order, flip, gst)


def unselect_body(ro, rb, own, oth, out):
    slots = lax.broadcasted_iota(jnp.int32, (ROWS, HALF), 0)
    pick_own = (slots == ro[...]).astype(F32).astype(BF)
    pick_back = (slots == rb[...]).astype(F32).astype(BF)
    out[...] = (tn(pick_own, own[...]) + tn(pick_back, oth[...])).astype(BF)


def attend_body(assembled, *refs):
    if assembled:
        n1, w_in, bias, add, w, qkv, probs, ctx, att = refs
        w = w_in
    else:
        order, n1, own, oth, bias, add, w, qkv, probs, ctx, att = refs
        put_back(order, own, oth, w)
    values = nn(n1[...], w[:, :640]) + bias[...]
    qkv[...] = values.astype(BF)
    ctx[:, 0:64] = jnp.zeros((ROWS, 64), BF)
    for at, size, small in PARTS:
        cut = slice(at, at + size)
        for h in range(3):
            q = qkv[cut, h * 64 : h * 64 + 64]
            k = qkv[cut, 192 + h * 64 : 256 + h * 64]
            v = qkv[cut, 384 + h * 64 : 448 + h * 64]
            p = probabilities(q, k, block_mask(size, small)).astype(BF)
            probs[h, cut, 0:size] = p
            ctx[cut, 64 + h * 64 : 128 + h * 64] = nn(p, v).astype(BF)
    att[...] = add[...] + nt(ctx[...], w[:, 512:768])


def middle_body(order, xs, att, vec, middle, n2, n2t, flip):
    mid = xs[...].astype(F32) + att[...] + vec[5:6, :]
    middle[...] = mid
    hat, _ = norm_stats(mid)
    normed = (hat * vec[2:3, :] + vec[3:4, :]).astype(BF)
    n2[...] = normed
    flip[...] = normed.T
    put_in_order(order, flip, n2t)


def hidden_body(assembled, *refs):
    if assembled:
        n2, gs, n2t, gst, w1, w2, bias, out_in, gn_in, *refs = refs
        keep, away, brow, out, gn, act, gb = refs
    else:
        order, n2, gs, n2t, gst, own, oth, bias, out_in, gn_in, *refs = refs
        keep, away, brow, out, gn, act, gb, w1, w2 = refs
        put_back(order, own, oth, w1)
        put_back(order, own, oth, w2, 96)
    for at in range(0, D, 256):
        cut = slice(at, at + 256)
        before = nn(n2[...], w1[:, cut]) + bias[0:1, cut]
        cdf = 0.5 + 0.5 * lax.erf(before * (0.5**0.5))
        act[:, cut] = (before * cdf).astype(BF)
        slope = cdf + before * jnp.exp(-0.5 * before * before) * 0.3989422804014327
        grad = (nt(gs[...], w2[cut, :]) * slope).astype(BF)
        gb[:, cut] = grad
        brow[:, cut] = jnp.sum(grad.astype(F32), axis=0, keepdims=True)
    out[...] = out_in[...] + nn(act[...], w2[...])
    gn[...] = gn_in[...] + nt(gb[...], w1[...])
    for half, target in ((0, keep), (384, away)):
        first = nn(n2t[half : half + 384, :], gb[...]).astype(BF)
        second = nn(gst[half : half + 384, :], act[...]).astype(BF)
        for j in range(4):
            target[j, 0:96, :] = first[96 * j : 96 * j + 96]
            target[j, 96:192, :] = second[96 * j : 96 * j + 96]


def turn_body(order, middle, ffn, gn2, gs, vec, rows_out, gm, ga, gat, sums, flip):
    mid = middle[...]
    rows_out[...] = (mid + ffn[...] + vec[6:7, :]).astype(BF)
    hat, scale = norm_stats(mid)
    grad = gn2[...]
    top = gs[...].astype(F32)
    total = top + norm_back(hat, scale, vec[2:3, :], grad)
    gm[...] = total
    low = total.astype(BF)
    ga[...] = low
    flip[...] = low.T
    put_in_order(order, flip, gat)
    sums[...] = jnp.zeros(sums.shape, F32)
    sums[0:1, :] = jnp.sum(low.astype(F32), axis=0, keepdims=True)
    sums[1:2, :] = jnp.sum(grad * hat, axis=0, keepdims=True)
    sums[2:3, :] = jnp.sum(grad, axis=0, keepdims=True)
    sums[3:4, :] = jnp.sum(top, axis=0, keepdims=True)


def attend_back_body(ga, gat, n1t, w, qkv, probs, ctx, gn_in, keep, away, brow, gn, gc, dqkv):
    gc[...] = nn(ga[...], w[:, 512:768]).astype(BF)
    dqkv[:, 576:640] = jnp.zeros((ROWS, 64), BF)
    for at, size, small in PARTS:
        cut = slice(at, at + size)
        for h in range(3):
            q = qkv[cut, h * 64 : h * 64 + 64]
            k = qkv[cut, 192 + h * 64 : 256 + h * 64]
            v = qkv[cut, 384 + h * 64 : 448 + h * 64]
            g = gc[cut, 64 + h * 64 : 128 + h * 64]
            low = probs[h, cut, 0:size]
            p = low.astype(F32)
            gp = nt(g, v)
            ds = (p * (gp - jnp.sum(p * gp, axis=-1, keepdims=True)) * 0.125).astype(BF)
            dqkv[cut, h * 64 : h * 64 + 64] = nn(ds, k).astype(BF)
            dqkv[cut, 192 + h * 64 : 256 + h * 64] = tn(ds, q).astype(BF)
            dqkv[cut, 384 + h * 64 : 448 + h * 64] = tn(low, g).astype(BF)
    grads = dqkv[...]
    brow[...] = jnp.sum(grads.astype(F32), axis=0, keepdims=True)
    gn[...] = gn_in[...] + nt(grads, w[:, :640])
    for half, target in ((0, keep), (384, away)):
        first = nn(n1t[half : half + 384, :], grads)
        second = nn(gat[half : half + 384, :], ctx[...])
        for j in range(4):
            cut = slice(96 * j, 96 * j + 96)
            target[j, :, 0:512] = first[cut, 0:512].astype(BF)
            target[j, :, 512:640] = (first[cut, 512:640] + second[cut, 0:128]).astype(BF)
            target[j, :, 640:768] = second[cut, 128:256].astype(BF)


def last_body(xs, gm, gn1, vec, rows_out, sums):
    hat, scale = norm_stats(xs[...].astype(F32))
    grad = gn1[...]
    rows_out[...] = (gm[...] + norm_back(hat, scale, vec[0:1, :], grad)).astype(BF)
    sums[...] = jnp.zeros(sums.shape, F32)
    sums[0:1, :] = jnp.sum(grad * hat, axis=0, keepdims=True)
    sums[1:2, :] = jnp.sum(grad, axis=0, keepdims=True)


def hidden_final_body(order, own, oth, first, second, flip):
    put_back(order, own, oth, first)
    put_back(order, own, oth, flip, 96)
    second[...] = flip[...].T


def attend_final_body(order, own, oth, qkv, out, full):
    put_back(order, own, oth, full)
    for i in range(3):
        qkv[i] = full[:, 192 * i : 192 * i + 192]
    out[...] = full[:, 512:768].T[64:256, :]


def local(routes, *args):
    (
        inputs, crop_labels, norm1_gain, norm1_bias, qkv_weight, qv_bias, out_weight, out_bias,
        norm2_gain, norm2_bias, fc1_weight, fc1_bias, fc2_weight, fc2_bias, cotangent,
    ) = args
    dp, z = lax.axis_index("dp"), lax.axis_index("mp")
    c, x, y = dp & 1, (dp >> 1) & 1, (dp >> 2) & 1
    quarter = y * 2 + x
    mp = routes.mp
    eye = list(range(mp))
    f = lambda t: t.astype(F32)

    def order_of(colour):
        near = jnp.where(colour == 0, 1, 2)
        far = 3 - near
        return [colour * 4 + (quarter ^ d) for d in (jnp.zeros_like(near), near, far, far + near)]

    order = jnp.stack(order_of(c) + order_of(1 - c)).astype(jnp.int32)

    wa0 = jnp.concatenate([qkv_weight[0], qkv_weight[1], qkv_weight[2], out_weight.T], axis=1)
    at = (c * 4 + quarter) * 96
    small_w = jnp.concatenate([fc1_bias, qv_bias[0], qv_bias[1]])
    small_w = jnp.pad(small_w, (0, 16 * D - small_w.shape[0])).reshape(16, D)
    piece_a = jnp.concatenate([lax.dynamic_slice_in_dim(wa0, at, 96), small_w])
    piece_f = jnp.concatenate(
        [lax.dynamic_slice_in_dim(t, at, 96) for t in (fc1_weight, fc2_weight)]
    )

    def spread(a0):
        a1 = send(a0, routes.first)
        pair = send(jnp.concatenate([a0, a1]), routes.second)
        own = jnp.concatenate([a0, a1, pair]).reshape(4, -1, D)
        return own, send(own, routes.core)

    got_a = [send(piece_a, routes.z[k]) for k in eye[1:]]
    got_f = [send(piece_f, routes.z[k]) for k in eye[1:]]
    spread_a = [spread(t[:96]) for t in got_a]
    spread_f = [spread(t) for t in got_f]
    smalls = [small_w] + [t[96:] for t in got_a]
    b1 = [f(t[0:1]) for t in smalls]
    nil = jnp.zeros((1, 192), F32)
    qkv_bias = [
        jnp.concatenate([f(t[1:2, :192]), nil, f(t[1:2, 192:384]), nil[:, :64]], axis=1)
        for t in smalls
    ]

    labels_here = crop_labels.reshape(-1, IMG_TOK)
    labels_there = send(labels_here, routes.core)
    labels = jnp.where((z & 1) == c, labels_here, labels_there)
    labels = lax.dynamic_index_in_dim(labels, z >> 1, axis=0, keepdims=False)
    row_here = targets(labels, c).reshape(2, HALF)
    row_there = targets(labels, 1 - c).reshape(2, HALF)
    row = lambda t, i: lax.dynamic_slice_in_dim(t, i, 1)
    row_own, row_oth, row_back = row(row_here, c), row(row_here, 1 - c), row(row_there, c)
    own_rows = send(jnp.stack([inputs, cotangent]), routes.image)
    oth_rows = send(own_rows, routes.core)
    vec = jnp.stack(
        [f(t) for t in (norm1_gain, norm1_bias, norm2_gain, norm2_bias, fc2_bias, out_bias, fc2_bias, fc2_bias)]
    )

    low, high, turned = ((ROWS, D), BF), ((ROWS, D), F32), ((D, ROWS), BF)
    flip = [pltpu.VMEM((D, ROWS), BF)]
    xs, gs, n1, n1t, gst = kernel(
        select_body, [low, low, low, turned, turned],
        [order, own_rows[0], oth_rows[0], own_rows[1], oth_rows[1], row_own, row_oth, vec],
        scratch=flip,
    )

    att = jnp.zeros((ROWS, D), F32)
    wa, qkv, probs, ctx = [], [], [], []
    shapes = [((D, D), BF), ((ROWS, 640), BF), ((3, ROWS, 256), BF), ((ROWS, 256), BF), high]
    for k in eye:
        if k == 0:
            weights, operands = wa0, [n1, wa0]
        else:
            operands = [order, n1, *spread_a[k - 1]]
        got = kernel(
            lambda *refs, k=k: attend_body(k == 0, *refs), shapes, operands + [qkv_bias[k], att]
        )
        wa.append(wa0 if k == 0 else got[0])
        qkv.append(got[1])
        probs.append(got[2])
        ctx.append(got[3])
        att = got[4]

    middle, n2, n2t = kernel(
        middle_body, [high, low, turned], [order, xs, att, vec], scratch=flip
    )

    ffn = gn2 = jnp.zeros((ROWS, D), F32)
    parts_f, b1_rows = [], []
    block = lambda n: ((4, n, D), BF)
    for k in eye:
        hold = [pltpu.VMEM((ROWS, D), BF)] * 2
        if k == 0:
            operands = [n2, gs, n2t, gst, fc1_weight, fc2_weight]
        else:
            operands = [order, n2, gs, n2t, gst, *spread_f[k - 1]]
            hold = hold + [pltpu.VMEM((D, D), BF)] * 2
        keep, away, brow, ffn, gn2 = kernel(
            lambda *refs, k=k: hidden_body(k == 0, *refs),
            [block(192), block(192), ((1, D), F32), high, high],
            operands + [b1[k], ffn, gn2],
            scratch=hold,
        )
        parts_f.append((keep, send(away, routes.core)))
        b1_rows.append(brow)

    def give(rows):
        there = send(rows, routes.core)
        (half,) = kernel(
            unselect_body, [((HALF, D), BF)], [row_own, row_back, rows, there]
        )
        return send(half, routes.image)

    def collect(parts):
        keep = [f(a) + f(b) for a, b in parts]
        got = send(jnp.stack([t[2:] for t in keep]).astype(BF), routes.second)
        keep = [t[:2] + f(g) for t, g in zip(keep, got)]
        got = send(jnp.stack([t[1] for t in keep]).astype(BF), routes.first)
        return [t[0] + f(g) for t, g in zip(keep, got)]

    def finish(parts):
        total = parts[0]
        for k in eye[1:]:
            total = total + f(send(parts[k].astype(BF), routes.z[k]))
        for route in routes.group:
            total = total + f(send(total.astype(BF), route))
        return spread(total.astype(BF))

    sums_f = collect(parts_f[:2]) + collect(parts_f[2:])
    fc1_grad, fc2_grad = kernel(
        hidden_final_body, [((D, D), F32)] * 2, [order, *finish(sums_f)],
        scratch=[pltpu.VMEM((D, D), F32)],
    )

    rows_out, gm, ga, gat, sums_one = kernel(
        turn_body, [low, high, low, turned, ((8, D), F32)],
        [order, middle, ffn, gn2, gs, vec], scratch=flip,
    )
    layer_out = give(rows_out)

    gn1 = jnp.zeros((ROWS, D), F32)
    parts_a, qkv_rows = [], []
    for k in eye:
        keep, away, brow, gn1 = kernel(
            attend_back_body, [block(96), block(96), ((1, 640), F32), high],
            [ga, gat, n1t, wa[k], qkv[k], probs[k], ctx[k], gn1],
            scratch=[pltpu.VMEM((ROWS, 256), BF), pltpu.VMEM((ROWS, 640), BF)],
        )
        parts_a.append((keep, send(away, routes.core)))
        qkv_rows.append(brow)
    rows_in, sums_two = kernel(last_body, [low, ((8, D), F32)], [xs, gm, gn1, vec])
    input_grad = give(rows_in)
    qkv_grad, out_grad = kernel(
        attend_final_body, [((3, D, 192), F32), ((192, D), F32)],
        [order, *finish(collect(parts_a))], scratch=[pltpu.VMEM((D, D), F32)],
    )

    def by_shard(rows):
        return choose(jnp.concatenate(rows), jnp.arange(mp) ^ z)

    sums = jnp.concatenate(
        [
            sums_two[0:2],
            sums_one[0:4],
            by_shard(b1_rows),
            by_shard([t[:, :192] for t in qkv_rows]).reshape(1, D),
            by_shard([t[:, 384:576] for t in qkv_rows]).reshape(1, D),
        ]
    )
    for route in [routes.core, routes.x, routes.y, routes.z[1], routes.z[2], *routes.group]:
        sums = sums + send(sums, route)
    width = D // mp
    return (
        layer_out,
        input_grad,
        sums[0],
        sums[1],
        qkv_grad,
        lax.dynamic_slice(sums[10:12], (0, z * width), (2, width)),
        out_grad,
        sums[2],
        sums[3],
        sums[4],
        fc1_grad,
        lax.dynamic_index_in_dim(sums, 6 + z, axis=0, keepdims=False),
        fc2_grad,
        sums[5],
    )


def solution(mesh):
    routes = Routes(mesh.shape["dp"], mesh.shape["mp"])
    placed = (
        P(ALL, None), P("dp"), P(), P(), P(None, None, "mp"), P(None, "mp"), P("mp", None), P(),
        P(), P(), P(None, "mp"), P("mp"), P("mp", None), P(), P(ALL, None),
    )
    given = (
        P(ALL, None), P(ALL, None), P(), P(), P(None, None, "mp"), P(None, "mp"), P("mp", None),
        P(), P(), P(), P(None, "mp"), P("mp"), P("mp", None), P(),
    )
    return jax.shard_map(
        lambda *args: local(routes, *args),
        mesh=mesh,
        in_specs=placed,
        out_specs=given,
        check_vma=False,
    )
```

```python
import jax
import jax.numpy as jnp
from jax import lax
from jax.experimental import pallas as pl
from jax.experimental.pallas import tpu as pltpu
from jax.sharding import PartitionSpec as P

HEAD_DIM = 64
IMG_TOK = 690
HALF = 345
BIG = 197
SMALL = 37
BIG_PAD = 208
ROWS = 368
D = 768
BF = jnp.bfloat16
F32 = jnp.float32
ALL = ("dp", "mp")


def nt(a, b):
    return lax.dot_general(a, b, (((1,), (1,)), ((), ())), preferred_element_type=F32)


def tn(a, b):
    return lax.dot_general(a, b, (((0,), (0,)), ((), ())), preferred_element_type=F32)


def nn(a, b):
    return lax.dot_general(a, b, (((1,), (0,)), ((), ())), preferred_element_type=F32)


class Routes:
    def __init__(self, dp, mp):
        self.dp, self.mp = dp, mp
        self.groups = dp // 8

        def table(move):
            pairs = []
            for d in range(dp):
                for z in range(mp):
                    g, y, x, c = d >> 3, (d >> 2) & 1, (d >> 1) & 1, d & 1
                    g2, y2, x2, c2, z2 = move(g, y, x, c, z)
                    pairs.append((d * mp + z, (g2 * 8 + y2 * 4 + x2 * 2 + c2) * mp + z2))
            return pairs

        self.core = table(lambda g, y, x, c, z: (g, y, x, 1 - c, z))
        self.first = table(
            lambda g, y, x, c, z: (g, y, 1 - x, c, z) if c == 0 else (g, 1 - y, x, c, z)
        )
        self.second = table(
            lambda g, y, x, c, z: (g, 1 - y, x, c, z) if c == 0 else (g, y, 1 - x, c, z)
        )
        self.x = table(lambda g, y, x, c, z: (g, y, 1 - x, c, z))
        self.y = table(lambda g, y, x, c, z: (g, 1 - y, x, c, z))
        self.z = [table(lambda g, y, x, c, z, k=k: (g, y, x, c, z ^ k)) for k in range(mp)]
        self.image = table(
            lambda g, y, x, c, z: (g, y, x, 1 - c, z ^ 1) if c != (z & 1) else (g, y, x, c, z)
        )
        self.group = [
            table(lambda g, y, x, c, z, b=b: (g ^ b, y, x, c, z))
            for b in (1 << i for i in range(max(self.groups.bit_length() - 1, 0)))
        ]


def send(value, route):
    return lax.ppermute(value, ALL, route)


def after(value, *others):
    return lax.optimization_barrier((value, *others))[0]


def choose(stack, places):
    return jnp.stack([lax.dynamic_index_in_dim(stack, i, keepdims=False) for i in places])


def norm_stats(values):
    average = jnp.mean(values, axis=-1, keepdims=True)
    centred = values - average
    spread = jnp.mean(centred * centred, axis=-1, keepdims=True)
    scale = lax.rsqrt(spread + 1e-06)
    return centred * scale, scale


def norm_back(hat, scale, gain, grad):
    inner = grad * gain
    a = jnp.mean(inner, axis=-1, keepdims=True)
    b = jnp.mean(inner * hat, axis=-1, keepdims=True)
    return scale * (inner - a - hat * b)


def block_mask(size, small):
    i = lax.broadcasted_iota(jnp.int32, (size, size), 0)
    j = lax.broadcasted_iota(jnp.int32, (size, size), 1)
    if not small:
        return j < BIG
    return (i // SMALL == j // SMALL) & (j < 4 * SMALL)


def probabilities(q, k, mask):
    logits = jnp.where(mask, nt(q, k) * 0.125, -1e9)
    e = jnp.exp(logits - jnp.max(logits, axis=-1, keepdims=True))
    return e / jnp.sum(e, axis=-1, keepdims=True)


PARTS = ((0, BIG_PAD, False), (BIG_PAD, ROWS - BIG_PAD, True))


def targets(labels, c):
    crops = jnp.arange(10, dtype=jnp.int32)
    member = labels[:, None] == crops[None, :]
    ahead = (crops[None, :] < crops[:, None]).astype(jnp.int32)
    count = jnp.sum(member.astype(jnp.int32), axis=0)
    big = (count > 100).astype(jnp.int32)
    start = jnp.sum(ahead * count[None, :], axis=1)
    rank_big = jnp.sum(ahead * big[None, :], axis=1)
    rank_small = jnp.sum(ahead * (1 - big)[None, :], axis=1)
    core = jnp.where(big == 1, rank_big, rank_small // 4)
    base = jnp.where(big == 1, 0, BIG_PAD + (rank_small % 4) * SMALL)
    shift = jnp.where(core == c, base - start, -100000)
    place = jnp.arange(labels.shape[0], dtype=jnp.int32)
    row = place + jnp.sum(jnp.where(member, shift[None, :], 0), axis=1)
    return jnp.where(row < 0, -1, row)


def kernel(body, outs, args, us, scratch=()):
    vmem = pl.BlockSpec(memory_space=pltpu.VMEM)
    smem = pl.BlockSpec(memory_space=pltpu.SMEM)
    return pl.pallas_call(
        body,
        out_shape=tuple(jax.ShapeDtypeStruct(shape, kind) for shape, kind in outs),
        in_specs=[smem if a.ndim == 1 else vmem for a in args],
        out_specs=tuple(vmem for _ in outs),
        scratch_shapes=list(scratch),
        compiler_params=pltpu.CompilerParams(vmem_limit_bytes=24 << 20),
        cost_estimate=pl.CostEstimate(
            flops=int(us * 1.15e9), bytes_accessed=0, transcendentals=0
        ),
    )(*args)


def put_in_order(order, source, out):
    for j in range(8):
        at = pl.multiple_of(order[j] * 96, 96)
        out[96 * j : 96 * j + 96, :] = source[pl.ds(at, 96), :]


def put_back(order, own, oth, out, first=0, size=96):
    for j in range(8):
        at = pl.multiple_of(order[j] * 96, 96)
        part = (own, oth)[j // 4][j % 4, first : first + size, :]
        out[pl.ds(at, size), :] = part.astype(out.dtype)


def select_body(own, oth, ro, rt, vec, xs, n1):
    slots = lax.broadcasted_iota(jnp.int32, (ROWS, HALF), 0)
    pick_own = (slots == ro[...]).astype(F32).astype(BF)
    pick_oth = (slots == rt[...]).astype(F32).astype(BF)
    rows = nn(pick_own, own[...]) + nn(pick_oth, oth[...])
    xs[...] = rows.astype(BF)
    hat, _ = norm_stats(rows)
    normed = hat * vec[0:1, :] + vec[1:2, :]
    n1[...] = normed.astype(BF)


def select_top_body(order, own, oth, ro, rt, gs, gst, flip):
    slots = lax.broadcasted_iota(jnp.int32, (ROWS, HALF), 0)
    pick_own = (slots == ro[...]).astype(F32).astype(BF)
    pick_oth = (slots == rt[...]).astype(F32).astype(BF)
    grads = (nn(pick_own, own[...]) + nn(pick_oth, oth[...])).astype(BF)
    gs[...] = grads
    flip[...] = grads.T
    put_in_order(order, flip, gst)


def unselect_body(ro, rb, own, oth, out):
    slots = lax.broadcasted_iota(jnp.int32, (ROWS, HALF), 0)
    pick_own = (slots == ro[...]).astype(F32).astype(BF)
    pick_back = (slots == rb[...]).astype(F32).astype(BF)
    out[...] = (tn(pick_own, own[...]) + tn(pick_back, oth[...])).astype(BF)


def attend_body(assembled, *refs):
    if assembled:
        n1, w, bias, add, qkv, probs, ctx, att = refs
    else:
        order, n1, own, oth, bias, add, qkv, probs, ctx, att, w = refs
        put_back(order, own, oth, w)
    values = nt(n1[...], w[0:576, :]) + bias[...]
    qkv[...] = values.astype(BF)
    for at, size, small in PARTS:
        cut = slice(at, at + size)
        for h in range(3):
            q = qkv[cut, h * 64 : h * 64 + 64]
            k = qkv[cut, 192 + h * 64 : 256 + h * 64]
            v = qkv[cut, 384 + h * 64 : 448 + h * 64]
            p = probabilities(q, k, block_mask(size, small)).astype(BF)
            probs[h, cut, 0:size] = p
            ctx[cut, h * 64 : h * 64 + 64] = nn(p, v).astype(BF)
    att[...] = add[...] + nn(ctx[...], w[576:768, :])


def middle_body(order, xs, att, vec, middle, n2, n2t, flip):
    mid = xs[...].astype(F32) + att[...] + vec[5:6, :]
    middle[...] = mid
    hat, _ = norm_stats(mid)
    normed = (hat * vec[2:3, :] + vec[3:4, :]).astype(BF)
    n2[...] = normed
    flip[...] = normed.T
    put_in_order(order, flip, n2t)


def hidden_body(assembled, *refs):
    if assembled:
        n2, gs, n2t, gst, w1, w2, bias, out_in, gn_in, *refs = refs
        keep, away, brow, out, gn, act, gb = refs
    else:
        order, n2, gs, n2t, gst, own, oth, bias, out_in, gn_in, *refs = refs
        keep, away, brow, out, gn, act, gb, w1, w2 = refs
        put_back(order, own, oth, w1)
        put_back(order, own, oth, w2, 96)
    for at in range(0, D, 256):
        cut = slice(at, at + 256)
        before = nn(n2[...], w1[:, cut]) + bias[0:1, cut]
        cdf = 0.5 + 0.5 * lax.erf(before * (0.5**0.5))
        act[:, cut] = (before * cdf).astype(BF)
        slope = cdf + before * jnp.exp(-0.5 * before * before) * 0.3989422804014327
        grad = (nt(gs[...], w2[cut, :]) * slope).astype(BF)
        gb[:, cut] = grad
        brow[:, cut] = jnp.sum(grad.astype(F32), axis=0, keepdims=True)
    out[...] = out_in[...] + nn(act[...], w2[...])
    gn[...] = gn_in[...] + nt(gb[...], w1[...])
    for half, target in ((0, keep), (384, away)):
        first = nn(n2t[half : half + 384, :], gb[...]).astype(BF)
        second = nn(gst[half : half + 384, :], act[...]).astype(BF)
        for j in range(4):
            target[j, 0:96, :] = first[96 * j : 96 * j + 96]
            target[j, 96:192, :] = second[96 * j : 96 * j + 96]


def turn_body(middle, ffn, gn2, gs, vec, rows_out, gm, ga, sums):
    mid = middle[...]
    rows_out[...] = (mid + ffn[...] + vec[6:7, :]).astype(BF)
    hat, scale = norm_stats(mid)
    grad = gn2[...]
    top = gs[...].astype(F32)
    total = top + norm_back(hat, scale, vec[2:3, :], grad)
    gm[...] = total
    low = total.astype(BF)
    ga[...] = low
    sums[...] = jnp.zeros(sums.shape, F32)
    sums[0:1, :] = jnp.sum(low.astype(F32), axis=0, keepdims=True)
    sums[1:2, :] = jnp.sum(grad * hat, axis=0, keepdims=True)
    sums[2:3, :] = jnp.sum(grad, axis=0, keepdims=True)
    sums[3:4, :] = jnp.sum(top, axis=0, keepdims=True)


def attend_back_body(assembled, *refs):
    order, ga, n1, *refs = refs
    if assembled:
        w, qkv, probs, ctx, gn_in, keep, away, brow, gn, gc, dqkv, full = refs
    else:
        own, oth, qkv, probs, ctx, gn_in, keep, away, brow, gn, gc, dqkv, full, w = refs
        put_back(order, own, oth, w)
    gc[...] = nt(ga[...], w[576:768, :]).astype(BF)
    for at, size, small in PARTS:
        cut = slice(at, at + size)
        for h in range(3):
            q = qkv[cut, h * 64 : h * 64 + 64]
            k = qkv[cut, 192 + h * 64 : 256 + h * 64]
            v = qkv[cut, 384 + h * 64 : 448 + h * 64]
            g = gc[cut, h * 64 : h * 64 + 64]
            low = probs[h, cut, 0:size]
            p = low.astype(F32)
            gp = nt(g, v)
            ds = (p * (gp - jnp.sum(p * gp, axis=-1, keepdims=True)) * 0.125).astype(BF)
            dqkv[cut, h * 64 : h * 64 + 64] = nn(ds, k).astype(BF)
            dqkv[cut, 192 + h * 64 : 256 + h * 64] = tn(ds, q).astype(BF)
            dqkv[cut, 384 + h * 64 : 448 + h * 64] = tn(low, g).astype(BF)
    grads = dqkv[...]
    brow[...] = jnp.sum(grads.astype(F32), axis=0, keepdims=True)
    full[0:576, :] = tn(grads, n1[...]).astype(BF)
    full[576:768, :] = tn(ctx[...], ga[...]).astype(BF)
    for j in range(8):
        at = pl.multiple_of(order[j] * 96, 96)
        (keep, away)[j // 4][j % 4, :, :] = full[pl.ds(at, 96), :]
    gn[...] = gn_in[...] + nn(grads, w[0:576, :])


def last_body(order, xs, gm, gn1, vec, one, *refs):
    b1_rows, qkv_rows, rows_out, sums = refs[:4], refs[4:8], refs[8], refs[9]
    hat, scale = norm_stats(xs[...].astype(F32))
    grad = gn1[...]
    rows_out[...] = (gm[...] + norm_back(hat, scale, vec[0:1, :], grad)).astype(BF)
    sums[...] = jnp.zeros(sums.shape, F32)
    sums[0:1, :] = jnp.sum(grad * hat, axis=0, keepdims=True)
    sums[1:2, :] = jnp.sum(grad, axis=0, keepdims=True)
    sums[2:6, :] = one[0:4, :]
    for k in range(4):
        shard = order[8] ^ k
        sums[pl.ds(6 + shard, 1), :] = b1_rows[k][...]
        sums[pl.ds(10 + shard, 1), 0:576] = qkv_rows[k][...]


def hidden_final_body(order, own, oth, first, second, flip):
    put_back(order, own, oth, first)
    put_back(order, own, oth, flip, 96)
    second[...] = flip[...].T


def attend_final_body(order, own, oth, qkv, out, full):
    put_back(order, own, oth, full)
    for i in range(3):
        qkv[i] = full[192 * i : 192 * i + 192, :]
    out[...] = full[576:768, :]


def local(routes, *args):
    (
        inputs, crop_labels, norm1_gain, norm1_bias, qkv_weight, qv_bias, out_weight, out_bias,
        norm2_gain, norm2_bias, fc1_weight, fc1_bias, fc2_weight, fc2_bias, cotangent,
    ) = args
    dp, z = lax.axis_index("dp"), lax.axis_index("mp")
    c, x, y = dp & 1, (dp >> 1) & 1, (dp >> 2) & 1
    quarter = y * 2 + x
    mp = routes.mp
    eye = list(range(mp))
    f = lambda t: t.astype(F32)

    def order_of(colour):
        near = jnp.where(colour == 0, 1, 2)
        far = 3 - near
        return [colour * 4 + (quarter ^ d) for d in (jnp.zeros_like(near), near, far, far + near)]

    order = jnp.stack(order_of(c) + order_of(1 - c) + [z]).astype(jnp.int32)

    wa0 = jnp.concatenate([jnp.swapaxes(qkv_weight, 1, 2).reshape(-1, D), out_weight])
    at = (c * 4 + quarter) * 96
    small_w = jnp.concatenate([fc1_bias, qv_bias[0], qv_bias[1]])
    small_w = jnp.pad(small_w, (0, 16 * D - small_w.shape[0])).reshape(16, D)
    piece_a = jnp.concatenate([lax.dynamic_slice_in_dim(wa0, at, 96), small_w])
    piece_f = jnp.concatenate(
        [lax.dynamic_slice_in_dim(t, at, 96) for t in (fc1_weight, fc2_weight)]
    )

    def step_two(a0, a1):
        return send(jnp.concatenate([a0, a1]), routes.second)

    def step_three(a0, a1, pair):
        own = jnp.concatenate([a0, a1, pair]).reshape(4, -1, D)
        return own, send(own, routes.core)

    def spread(a0):
        a1 = send(a0, routes.first)
        return step_three(a0, a1, step_two(a0, a1))

    got_a = [send(piece_a, routes.z[k]) for k in eye[1:]]
    own_x = send(inputs, routes.image)
    got_f = [send(piece_f, routes.z[k]) for k in eye[1:]]
    own_g = send(cotangent, routes.image)
    a0 = [t[:96] for t in got_a]
    a1 = [send(t, routes.first) for t in a0]
    a2 = [step_two(s, t) for s, t in zip(a0, a1)]
    oth_x = send(after(own_x, *a1), routes.core)
    gates = [a1[2], a2[0], a2[1]]
    f1 = [send(after(t, g), routes.first) for t, g in zip(got_f, gates)]
    spread_a = [step_three(*t) for t in zip(a0, a1, a2)]
    f2 = [step_two(after(s, a2[2]), t) for s, t in zip(got_f, f1)]
    oth_g = send(after(own_g, f2[0]), routes.core)
    spread_f = [step_three(*t) for t in zip(got_f, f1, f2)]
    smalls = [small_w] + [t[96:] for t in got_a]
    b1 = [f(t[0:1]) for t in smalls]
    nil = jnp.zeros((1, 192), F32)
    qkv_bias = [
        jnp.concatenate([f(t[1:2, :192]), nil, f(t[1:2, 192:384])], axis=1)
        for t in smalls
    ]

    labels_here = crop_labels.reshape(-1, IMG_TOK)
    labels_there = send(labels_here, routes.core)
    labels = jnp.where((z & 1) == c, labels_here, labels_there)
    labels = lax.dynamic_index_in_dim(labels, z >> 1, axis=0, keepdims=False)
    row_here = targets(labels, c).reshape(2, HALF)
    row_there = targets(labels, 1 - c).reshape(2, HALF)
    row = lambda t, i: lax.dynamic_slice_in_dim(t, i, 1)
    row_own, row_oth, row_back = row(row_here, c), row(row_here, 1 - c), row(row_there, c)
    vec = jnp.stack(
        [f(t) for t in (norm1_gain, norm1_bias, norm2_gain, norm2_bias, fc2_bias, out_bias, fc2_bias, fc2_bias)]
    )

    low, high, turned = ((ROWS, D), BF), ((ROWS, D), F32), ((D, ROWS), BF)
    flip = [pltpu.VMEM((D, ROWS), BF)]
    xs, n1 = kernel(select_body, [low, low], [own_x, oth_x, row_own, row_oth, vec], 1.5)
    gs, gst = kernel(
        select_top_body, [low, turned], [order, own_g, oth_g, row_own, row_oth], 1.5, scratch=flip
    )

    att = jnp.zeros((ROWS, D), F32)
    qkv, probs, ctx = [], [], []
    shapes = [((ROWS, 576), BF), ((3, ROWS, 256), BF), ((ROWS, 192), BF), high]
    whole = [pltpu.VMEM((D, D), BF)]
    for k in eye:
        operands = [n1, wa0] if k == 0 else [order, n1, *spread_a[k - 1]]
        got = kernel(
            lambda *refs, k=k: attend_body(k == 0, *refs),
            shapes, operands + [qkv_bias[k], att], 3.0, scratch=whole if k else (),
        )
        qkv.append(got[0])
        probs.append(got[1])
        ctx.append(got[2])
        att = got[3]

    middle, n2, n2t = kernel(
        middle_body, [high, low, turned], [order, xs, att, vec], 1.1, scratch=flip
    )

    class Sum:
        def __init__(self, keep, away, slot):
            self.keep, self.slot = keep, slot
            self.core = send(away, routes.core)

        def far(self):
            pay = (f(self.keep[2:]) + f(self.core[2:])).astype(BF)
            self.far_in = send(pay, routes.second)
            return pay

        def near(self):
            pay = (f(self.keep[1]) + f(self.core[1]) + f(self.far_in[1])).astype(BF)
            self.near_in = send(pay, routes.first)
            return pay

        def home(self):
            pay = f(self.keep[0]) + f(self.core[0]) + f(self.far_in[0]) + f(self.near_in)
            pay = pay.astype(BF)
            self.result = send(pay, routes.z[self.slot]) if self.slot else pay
            return pay

    def gather_up(sums, gate):
        total = sum(f(after(s.result, gate)) for s in sums)
        for route in routes.group:
            total = total + f(send(total.astype(BF), route))
        return spread(total.astype(BF))

    ffn = gn2 = jnp.zeros((ROWS, D), F32)
    parts_f, b1_rows = [], []
    block = lambda n: ((4, n, D), BF)
    for k in eye:
        hold = [pltpu.VMEM((ROWS, D), BF)] * 2
        if k == 0:
            operands = [n2, gs, n2t, gst, fc1_weight, fc2_weight]
        else:
            operands = [order, n2, gs, n2t, gst, *spread_f[k - 1]]
            hold = hold + [pltpu.VMEM((D, D), BF)] * 2
        keep, away, brow, ffn, gn2 = kernel(
            lambda *refs, k=k: hidden_body(k == 0, *refs),
            [block(192), block(192), ((1, D), F32), high, high],
            operands + [b1[k], ffn, gn2],
            4.0,
            scratch=hold,
        )
        parts_f.append(Sum(keep, away, k))
        b1_rows.append(brow)
        if k in (1, 2):
            n2 = after(n2, parts_f[k - 1].far())

    def unselect(rows, there):
        return kernel(
            unselect_body, [((HALF, D), BF)], [row_own, row_back, rows, there], 1.5
        )[0]

    rows_out, gm, ga, sums_one = kernel(
        turn_body, [low, high, low, ((8, D), F32)], [middle, ffn, gn2, gs, vec], 1.7
    )
    ga = after(ga, parts_f[2].far(), parts_f[0].near())

    out_there = send(rows_out, routes.core)
    gn1 = jnp.zeros((ROWS, D), F32)
    parts_a, qkv_rows = [None] * mp, [None] * mp
    for k in reversed(eye):
        keep, away, brow, gn1 = kernel(
            lambda *refs, k=k: attend_back_body(k == 0, *refs),
            [block(96), block(96), ((1, 576), F32), high],
            [order, ga, n1, *([wa0] if k == 0 else spread_a[k - 1]), qkv[k], probs[k], ctx[k], gn1],
            4.5,
            scratch=[
                pltpu.VMEM((ROWS, 192), BF), pltpu.VMEM((ROWS, 576), BF), pltpu.VMEM((D, D), BF),
                *(whole if k else []),
            ],
        )
        parts_a[k] = Sum(keep, away, k)
        qkv_rows[k] = brow
        if k == 3:
            ga = after(ga, parts_f[3].far(), parts_f[1].near())
        if k == 2:
            half = unselect(rows_out, out_there)
            ga = after(ga, parts_a[3].far(), parts_f[2].near(), parts_f[0].home(), half)
        if k == 1:
            ga = after(ga, parts_a[2].far(), parts_f[3].near(), parts_f[1].home())
    layer_out = send(half, routes.image)
    rows_in, sums = kernel(
        last_body, [low, ((16, D), F32)],
        [order, xs, gm, gn1, vec, sums_one, *b1_rows, *qkv_rows], 1.2,
    )
    in_there = send(rows_in, routes.core)
    parts_f[2].home()
    parts_a[1].far()
    parts_a[3].near()
    parts_f[3].home()
    parts_a[0].far()
    parts_a[2].near()
    parts_a[3].home()
    parts_a[1].near()
    parts_a[2].home()
    parts_a[0].near()
    parts_a[1].home()
    parts_a[0].home()
    input_grad = send(unselect(rows_in, in_there), routes.image)
    fc1_grad, fc2_grad = kernel(
        hidden_final_body, [((D, D), F32)] * 2, [order, *gather_up(parts_f, gn1)], 3.0,
        scratch=[pltpu.VMEM((D, D), F32)],
    )
    qkv_grad, out_grad = kernel(
        attend_final_body, [((3, 192, D), F32), ((192, D), F32)],
        [order, *gather_up(parts_a, gn1)], 2.0, scratch=[pltpu.VMEM((D, D), F32)],
    )

    for route in [routes.core, routes.x, routes.y, routes.z[1], routes.z[2], *routes.group]:
        sums = sums + send(sums, route)
    qv_row = lax.dynamic_index_in_dim(sums, 10 + z, axis=0, keepdims=False)
    return (
        layer_out,
        input_grad,
        sums[0],
        sums[1],
        jnp.swapaxes(qkv_grad, 1, 2),
        jnp.stack([qv_row[:192], qv_row[384:576]]),
        out_grad,
        sums[2],
        sums[3],
        sums[4],
        fc1_grad,
        lax.dynamic_index_in_dim(sums, 6 + z, axis=0, keepdims=False),
        fc2_grad,
        sums[5],
    )


def solution(mesh):
    routes = Routes(mesh.shape["dp"], mesh.shape["mp"])
    placed = (
        P(ALL, None), P("dp"), P(), P(), P(None, None, "mp"), P(None, "mp"), P("mp", None), P(),
        P(), P(), P(None, "mp"), P("mp"), P("mp", None), P(), P(ALL, None),
    )
    given = (
        P(ALL, None), P(ALL, None), P(), P(), P(None, None, "mp"), P(None, "mp"), P("mp", None),
        P(), P(), P(), P(None, "mp"), P("mp"), P("mp", None), P(),
    )
    return jax.shard_map(
        lambda *args: local(routes, *args),
        mesh=mesh,
        in_specs=placed,
        out_specs=given,
        check_vma=False,
    )
```

```python
import jax
import jax.numpy as jnp
from jax import lax
from jax.experimental import pallas as pl
from jax.experimental.pallas import tpu as pltpu
from jax.sharding import PartitionSpec as P

HEAD_DIM = 64
IMG_TOK = 690
HALF = 345
BIG = 197
SMALL = 37
BIG_PAD = 208
ROWS = 368
D = 768
BF = jnp.bfloat16
F32 = jnp.float32
ALL = ("dp", "mp")


def nt(a, b):
    return lax.dot_general(a, b, (((1,), (1,)), ((), ())), preferred_element_type=F32)


def tn(a, b):
    return lax.dot_general(a, b, (((0,), (0,)), ((), ())), preferred_element_type=F32)


def nn(a, b):
    return lax.dot_general(a, b, (((1,), (0,)), ((), ())), preferred_element_type=F32)


class Routes:
    def __init__(self, dp, mp):
        self.dp, self.mp = dp, mp
        self.groups = dp // 8

        def table(move):
            pairs = []
            for d in range(dp):
                for z in range(mp):
                    g, y, x, c = d >> 3, (d >> 2) & 1, (d >> 1) & 1, d & 1
                    g2, y2, x2, c2, z2 = move(g, y, x, c, z)
                    pairs.append((d * mp + z, (g2 * 8 + y2 * 4 + x2 * 2 + c2) * mp + z2))
            return pairs

        self.core = table(lambda g, y, x, c, z: (g, y, x, 1 - c, z))
        self.first = table(
            lambda g, y, x, c, z: (g, y, 1 - x, c, z) if c == 0 else (g, 1 - y, x, c, z)
        )
        self.second = table(
            lambda g, y, x, c, z: (g, 1 - y, x, c, z) if c == 0 else (g, y, 1 - x, c, z)
        )
        self.x = table(lambda g, y, x, c, z: (g, y, 1 - x, c, z))
        self.y = table(lambda g, y, x, c, z: (g, 1 - y, x, c, z))
        self.z = [table(lambda g, y, x, c, z, k=k: (g, y, x, c, z ^ k)) for k in range(mp)]
        self.image = table(
            lambda g, y, x, c, z: (g, y, x, 1 - c, z ^ 1) if c != (z & 1) else (g, y, x, c, z)
        )
        self.group = [
            table(lambda g, y, x, c, z, b=b: (g ^ b, y, x, c, z))
            for b in (1 << i for i in range(max(self.groups.bit_length() - 1, 0)))
        ]


def send(value, route):
    return lax.ppermute(value, ALL, route)


def after(value, *others):
    return lax.optimization_barrier((value, *others))[0]


def choose(stack, places):
    return jnp.stack([lax.dynamic_index_in_dim(stack, i, keepdims=False) for i in places])


def norm_stats(values):
    average = jnp.mean(values, axis=-1, keepdims=True)
    centred = values - average
    spread = jnp.mean(centred * centred, axis=-1, keepdims=True)
    scale = lax.rsqrt(spread + 1e-06)
    return centred * scale, scale


def norm_back(hat, scale, gain, grad):
    inner = grad * gain
    a = jnp.mean(inner, axis=-1, keepdims=True)
    b = jnp.mean(inner * hat, axis=-1, keepdims=True)
    return scale * (inner - a - hat * b)


def block_mask(size, small):
    i = lax.broadcasted_iota(jnp.int32, (size, size), 0)
    j = lax.broadcasted_iota(jnp.int32, (size, size), 1)
    if not small:
        return j < BIG
    return (i // SMALL == j // SMALL) & (j < 4 * SMALL)


PARTS = ((0, BIG_PAD, False), (BIG_PAD, ROWS - BIG_PAD, True))


def targets(labels, c):
    crops = jnp.arange(10, dtype=jnp.int32)
    member = labels[:, None] == crops[None, :]
    ahead = (crops[None, :] < crops[:, None]).astype(jnp.int32)
    count = jnp.sum(member.astype(jnp.int32), axis=0)
    big = (count > 100).astype(jnp.int32)
    start = jnp.sum(ahead * count[None, :], axis=1)
    rank_big = jnp.sum(ahead * big[None, :], axis=1)
    rank_small = jnp.sum(ahead * (1 - big)[None, :], axis=1)
    core = jnp.where(big == 1, rank_big, rank_small // 4)
    base = jnp.where(big == 1, 0, BIG_PAD + (rank_small % 4) * SMALL)
    shift = jnp.where(core == c, base - start, -100000)
    place = jnp.arange(labels.shape[0], dtype=jnp.int32)
    row = place + jnp.sum(jnp.where(member, shift[None, :], 0), axis=1)
    return jnp.where(row < 0, -1, row)


def kernel(body, outs, args, us, scratch=(), far=(), alias=None, out_far=False):
    vmem = pl.BlockSpec(memory_space=pltpu.VMEM)
    smem = pl.BlockSpec(memory_space=pltpu.SMEM)
    return pl.pallas_call(
        body,
        out_shape=tuple(jax.ShapeDtypeStruct(shape, kind) for shape, kind in outs),
        in_specs=[smem if a.ndim == 1 else pl.BlockSpec(memory_space=pl.ANY) if i in far else vmem for i, a in enumerate(args)],
        out_specs=tuple(pl.BlockSpec(memory_space=pl.ANY) if out_far else vmem for _ in outs),
        scratch_shapes=list(scratch),
        input_output_aliases={i % len(args): o for i, o in (alias or {}).items()},
        compiler_params=pltpu.CompilerParams(vmem_limit_bytes=24 << 20),
        cost_estimate=pl.CostEstimate(
            flops=int(us * 1.15e9), bytes_accessed=0, transcendentals=0
        ),
    )(*args)


def put_in_order(order, source, out):
    for j in range(8):
        at = pl.multiple_of(order[j] * 96, 96)
        out[96 * j : 96 * j + 96, :] = source[pl.ds(at, 96), :]


def put_back(order, own, oth, out, first=0, size=96):
    for j in range(8):
        at = pl.multiple_of(order[j] * 96, 96)
        part = (own, oth)[j // 4][j % 4, first : first + size, :]
        out[pl.ds(at, size), :] = part.astype(out.dtype)


def pieces_body(order, qkv, out, b1, qv, fc1, fc2, whole, piece_a, piece_f, sems):
    at = pl.multiple_of(order[0] * 96, 96)
    copies = [
        pltpu.make_async_copy(t.at[pl.ds(at, 96)], piece_f.at[pl.ds(96 * i, 96)], sems.at[i])
        for i, t in enumerate((fc1, fc2))
    ]
    for copy in copies:
        copy.start()
    whole[0:576, :] = qkv[...]
    whole[576:768, :] = out[...]
    piece_a[0:96, :] = whole[pl.ds(at, 96), :]
    row = lax.broadcasted_iota(jnp.int32, (16, D), 0)
    second = jnp.concatenate([qv[0:1, :], qv[1:2, :], qv[0:1, :], qv[1:2, :]], axis=1)
    piece_a[96:112, :] = jnp.where(row == 0, b1[...].astype(F32), second.astype(F32)).astype(BF)
    for copy in copies:
        copy.wait()


def copy_body(one, two, first, second):
    first[...] = one[...]
    second[...] = two[...]


def select_body(own, oth, ro, rt, vec, xs, n1):
    slots = lax.broadcasted_iota(jnp.int32, (ROWS, HALF), 0)
    pick_own = (slots == ro[...]).astype(F32).astype(BF)
    pick_oth = (slots == rt[...]).astype(F32).astype(BF)
    rows = nn(pick_own, own[...]) + nn(pick_oth, oth[...])
    xs[...] = rows.astype(BF)
    hat, _ = norm_stats(rows)
    normed = hat * vec[0:1, :] + vec[1:2, :]
    n1[...] = normed.astype(BF)


def select_top_body(order, own, oth, ro, rt, gs, gst, flip):
    slots = lax.broadcasted_iota(jnp.int32, (ROWS, HALF), 0)
    pick_own = (slots == ro[...]).astype(F32).astype(BF)
    pick_oth = (slots == rt[...]).astype(F32).astype(BF)
    grads = (nn(pick_own, own[...]) + nn(pick_oth, oth[...])).astype(BF)
    gs[...] = grads
    flip[...] = grads.T
    put_in_order(order, flip, gst)


def unselect_body(ro, rb, own, oth, out):
    slots = lax.broadcasted_iota(jnp.int32, (ROWS, HALF), 0)
    pick_own = (slots == ro[...]).astype(F32).astype(BF)
    pick_back = (slots == rb[...]).astype(F32).astype(BF)
    out[...] = (tn(pick_own, own[...]) + tn(pick_back, oth[...])).astype(BF)


def heads_of(ref, cut, first):
    return [ref[cut, first + 64 * h : first + 64 * h + 64] for h in range(3)]


def attend_body(assembled, *refs):
    if assembled:
        n1, w, small, add, qkv, probs, ctx, att = refs
    else:
        order, n1, own, oth, small, add, qkv, probs, ctx, att, w = refs
        put_back(order, own, oth, w)
    values = nt(n1[...], w[0:576, :])
    at = small.shape[0] - 15
    shift = small[at : at + 1, 0:384].astype(F32)
    qkv[:, 0:192] = (values[:, 0:192] + shift[:, 0:192]).astype(BF)
    qkv[:, 192:384] = values[:, 192:384].astype(BF)
    qkv[:, 384:576] = (values[:, 384:576] + shift[:, 192:384]).astype(BF)
    for at, size, block in PARTS:
        cut = slice(at, at + size)
        queries, keys, inner = (heads_of(qkv, cut, first) for first in (0, 192, 384))
        mask = block_mask(size, block)
        logits = [jnp.where(mask, nt(q, k) * 0.125, -1e9) for q, k in zip(queries, keys)]
        e = [jnp.exp(t - jnp.max(t, axis=-1, keepdims=True)) for t in logits]
        p = [(t / jnp.sum(t, axis=-1, keepdims=True)).astype(BF) for t in e]
        for h in range(3):
            probs[h, cut, 0:size] = p[h]
        ctx[cut, :] = jnp.concatenate([nn(s, v).astype(BF) for s, v in zip(p, inner)], axis=1)
    att[...] = add[...] + nn(ctx[...], w[576:768, :])


def middle_body(order, xs, att, vec, middle, n2, n2t, flip):
    mid = xs[...].astype(F32) + att[...] + vec[5:6, :]
    middle[...] = mid
    hat, _ = norm_stats(mid)
    normed = (hat * vec[2:3, :] + vec[3:4, :]).astype(BF)
    n2[...] = normed
    flip[...] = normed.T
    put_in_order(order, flip, n2t)


def hidden_body(assembled, *refs):
    if assembled:
        n2, gs, n2t, gst, w1, w2, small, out_in, gn_in, *refs = refs
        keep, away, brow, out, gn, act, gb = refs
    else:
        order, n2, gs, n2t, gst, own, oth, small, out_in, gn_in, *refs = refs
        keep, away, brow, out, gn, act, gb, w1, w2 = refs
        put_back(order, own, oth, w1)
        put_back(order, own, oth, w2, 96)
    at = small.shape[0] - 16
    shift = small[at : at + 1, :].astype(F32)
    for at in range(0, D, 256):
        cut = slice(at, at + 256)
        before = nn(n2[...], w1[:, cut]) + shift[:, cut]
        cdf = 0.5 + 0.5 * lax.erf(before * (0.5**0.5))
        act[:, cut] = (before * cdf).astype(BF)
        slope = cdf + before * jnp.exp(-0.5 * before * before) * 0.3989422804014327
        grad = (nt(gs[...], w2[cut, :]) * slope).astype(BF)
        gb[:, cut] = grad
        brow[:, cut] = jnp.sum(grad.astype(F32), axis=0, keepdims=True)
    out[...] = out_in[...] + nn(act[...], w2[...])
    gn[...] = gn_in[...] + nt(gb[...], w1[...])
    for half, target in ((0, keep), (384, away)):
        first = nn(n2t[half : half + 384, :], gb[...]).astype(BF)
        second = nn(gst[half : half + 384, :], act[...]).astype(BF)
        for j in range(4):
            target[j, 0:96, :] = first[96 * j : 96 * j + 96]
            target[j, 96:192, :] = second[96 * j : 96 * j + 96]


def turn_body(middle, ffn, gn2, gs, vec, rows_out, gm, ga, sums):
    mid = middle[...]
    rows_out[...] = (mid + ffn[...] + vec[6:7, :]).astype(BF)
    hat, scale = norm_stats(mid)
    grad = gn2[...]
    top = gs[...].astype(F32)
    total = top + norm_back(hat, scale, vec[2:3, :], grad)
    gm[...] = total
    low = total.astype(BF)
    ga[...] = low
    sums[...] = jnp.zeros(sums.shape, F32)
    sums[0:1, :] = jnp.sum(low.astype(F32), axis=0, keepdims=True)
    sums[1:2, :] = jnp.sum(grad * hat, axis=0, keepdims=True)
    sums[2:3, :] = jnp.sum(grad, axis=0, keepdims=True)
    sums[3:4, :] = jnp.sum(top, axis=0, keepdims=True)


def attend_back_body(assembled, *refs):
    order, ga, n1, *refs = refs
    if assembled:
        w, qkv, probs, ctx, gn_in, keep, away, brow, gn, gc, dqkv, full = refs
    else:
        own, oth, qkv, probs, ctx, gn_in, keep, away, brow, gn, gc, dqkv, full, w = refs
        put_back(order, own, oth, w)
    gc[...] = nt(ga[...], w[576:768, :]).astype(BF)
    for at, size, _ in PARTS:
        cut = slice(at, at + size)
        queries, keys, inner = (heads_of(qkv, cut, first) for first in (0, 192, 384))
        tops = heads_of(gc, cut, 0)
        low = [probs[h, cut, 0:size] for h in range(3)]
        p = [t.astype(F32) for t in low]
        gp = [nt(g, v) for g, v in zip(tops, inner)]
        ds = [
            (a * (b - jnp.sum(a * b, axis=-1, keepdims=True)) * 0.125).astype(BF)
            for a, b in zip(p, gp)
        ]
        dv = [tn(a, g).astype(BF) for a, g in zip(low, tops)]
        dq = [nn(a, k).astype(BF) for a, k in zip(ds, keys)]
        dk = [tn(a, q).astype(BF) for a, q in zip(ds, queries)]
        dqkv[cut, :] = jnp.concatenate(dq + dk + dv, axis=1)
    grads = dqkv[...]
    brow[...] = jnp.sum(grads.astype(F32), axis=0, keepdims=True)
    full[0:576, :] = tn(grads, n1[...]).astype(BF)
    full[576:768, :] = tn(ctx[...], ga[...]).astype(BF)
    for j in range(8):
        at = pl.multiple_of(order[j] * 96, 96)
        (keep, away)[j // 4][j % 4, :, :] = full[pl.ds(at, 96), :]
    gn[...] = gn_in[...] + nn(grads, w[0:576, :])


def last_body(order, xs, gm, gn1, vec, one, *refs):
    b1_rows, qkv_rows, rows_out, sums = refs[:4], refs[4:8], refs[8], refs[9]
    hat, scale = norm_stats(xs[...].astype(F32))
    grad = gn1[...]
    rows_out[...] = (gm[...] + norm_back(hat, scale, vec[0:1, :], grad)).astype(BF)
    sums[...] = jnp.zeros(sums.shape, F32)
    sums[0:1, :] = jnp.sum(grad * hat, axis=0, keepdims=True)
    sums[1:2, :] = jnp.sum(grad, axis=0, keepdims=True)
    sums[2:6, :] = one[0:4, :]
    for k in range(4):
        shard = order[8] ^ k
        sums[pl.ds(6 + shard, 1), :] = b1_rows[k][...]
        sums[pl.ds(10 + shard, 1), 0:576] = qkv_rows[k][...]


def hidden_final_body(order, own, oth, first, second, flat, flip, turned, sems):
    copies = []
    for j in range(8):
        at = pl.multiple_of(order[j] * 96, 96)
        part = (own, oth)[j // 4].at[j % 4]
        flat[96 * j : 96 * j + 96, :] = part[0:96, :].astype(F32)
        flip[pl.ds(at, 96), :] = part[96:192, :]
        copies.append(
            pltpu.make_async_copy(flat.at[pl.ds(96 * j, 96)], first.at[pl.ds(at, 96)], sems.at[j])
        )
        copies[-1].start()
    for i in range(6):
        cut = slice(128 * i, 128 * i + 128)
        turned[cut, :] = flip[:, cut].T.astype(F32)
        rows = pl.ds(128 * i, 128)
        copies.append(pltpu.make_async_copy(turned.at[rows], second.at[rows], sems.at[8 + i]))
        copies[-1].start()
    for copy in copies:
        copy.wait()


def attend_final_body(order, own, oth, qkv, out, full, sems):
    put_back(order, own, oth, full)
    copies = [
        pltpu.make_async_copy(full.at[pl.ds(192 * i, 192)], qkv.at[i] if i < 3 else out, sems.at[i])
        for i in range(4)
    ]
    for copy in copies:
        copy.start()
    for copy in copies:
        copy.wait()


GROUPS = {
    "ga": ((1,), (2,), (3,)),
    "gf": ((1,), (2,), (3,)),
    "f": ((0,), (1,), (2,), (3,)),
    "a": ((3,), (2,), (1,), (0,)),
}
HALVES = ()
COSTS = {
    "enda": 0.35,
    "attend2": 8.0,
    "hidden3": 8.0,
    "hidden0": 0.5,
    "back1": 0.8,
    "unout": 0.1,
    "unin": 8.0,
    "attend3": 2.0,
    "top": 0.7,
    "attend0": 0.07,
    "back2": 0.062,
    "copy": 2.0,
    "back3": 0.7,
}
BEFORE = {
    "f0far": "hidden2",
    "f1near": "back2",
    "gf1one": "attend1",
    "x": "attend1",
    "f2near": "last",
    "f0home": "enda",
    "xcore": "hidden0",
    "ga1one": "top",
    "f3near": "unout",
    "a1near": "enda",
    "a2home": "back0",
    "f0near": "back3",
    "a3far": "back1",
    "f2home": "unout",
    "f1far": "hidden3",
    "ga2own2": "back2",
    "a2far": "back0",
    "f3far": "back2",
    "f2far": "back3",
    "gf1two": "last",
}
AFTER = {
    "ga3z": "hidden1",
    "f0home": "turn",
    "hfone": "select",
    "g": "attend2",
    "f2home": "endf",
    "ga3two": "back0",
    "s3": "endf",
    "a0near": "top",
    "gf2one": "endf",
    "gcore": "attend0",
    "f1far": "back3",
    "haown": "top",
    "gf1own1": "unout",
    "gf3two": "back1",
    "a3far": "hidden0",
    "gf1one": "back0",
    "f1near": "hidden0",
    "a2far": "copy",
    "gf3one": "copy",
}


class Plan:
    def __init__(self):
        self.makers, self.values, self.outputs = {}, {}, {}

    def payload(self, name, make, route):
        self.makers[name] = (make, route)

    def get(self, name):
        if name not in self.values:
            make, route = self.makers[name]
            value = make()
            late = self.outputs.get(AFTER.get(name))
            if late is not None:
                value = after(value, late)
            self.values[name] = (value, value if route is None else send(value, route))
        return self.values[name]

    def arrived(self, name):
        return self.get(name)[1]

    def run(self, name, body, outs, args, us, scratch=(), hold=0, alias=None, out_far=False):
        gates = []
        for payload, late in BEFORE.items():
            if late == name:
                try:
                    gates.append(self.get(payload)[0])
                except KeyError:
                    pass
        args = list(args)
        if gates:
            args[hold] = after(args[hold], *gates)
        got = kernel(body, outs, args, us * COSTS.get(name, 1.0), scratch, (), alias, out_far)
        self.outputs[name] = got[-1]
        return got


def local(routes, *args):
    (
        inputs, crop_labels, norm1_gain, norm1_bias, qkv_weight, qv_bias, out_weight, out_bias,
        norm2_gain, norm2_bias, fc1_weight, fc1_bias, fc2_weight, fc2_bias, cotangent,
    ) = args
    dp, z = lax.axis_index("dp"), lax.axis_index("mp")
    c, x, y = dp & 1, (dp >> 1) & 1, (dp >> 2) & 1
    quarter = y * 2 + x
    mp = routes.mp
    eye = list(range(mp))
    f = lambda t: t.astype(F32)
    plan = Plan()

    def order_of(colour):
        near = jnp.where(colour == 0, 1, 2)
        far = 3 - near
        return [colour * 4 + (quarter ^ d) for d in (jnp.zeros_like(near), near, far, far + near)]

    order = jnp.stack(order_of(c) + order_of(1 - c) + [z]).astype(jnp.int32)

    wa0, piece_a, piece_f = kernel(
        pieces_body, [((D, D), BF), ((112, D), BF), ((192, D), BF)],
        [
            order, jnp.swapaxes(qkv_weight, 1, 2).reshape(-1, D), out_weight, fc1_bias[None], qv_bias,
            fc1_weight, fc2_weight,
        ],
        1.3, scratch=[pltpu.SemaphoreType.DMA((2,))], far=(5, 6),
    )

    owner = {}

    def legs(tag, slots, first, rows):
        def own(i):
            pair = [plan.get(tag + "two")[0][:, i], plan.arrived(tag + "two")[:, i]]
            return jnp.concatenate(pair)

        plan.payload(tag + "one", first, routes.first)
        plan.payload(
            tag + "two",
            lambda: jnp.stack([t[:, :rows] for t in plan.get(tag + "one")]),
            routes.second,
        )
        for i, k in enumerate(slots):
            owner[tag[:2], k] = f"{tag}own{k}"
            plan.payload(f"{tag}own{k}", lambda i=i: own(i), routes.core)

    for kind, piece, rows in (("ga", piece_a, 96), ("gf", piece_f, 192)):
        for k in eye[1:]:
            plan.payload(f"{kind}{k}z", lambda piece=piece: piece, routes.z[k])
        for slots in GROUPS[kind]:
            legs(
                kind + "".join(map(str, slots)), slots,
                lambda kind=kind, slots=slots: jnp.stack([plan.arrived(f"{kind}{k}z") for k in slots]),
                rows,
            )
    plan.payload("x", lambda: inputs, routes.image)
    plan.payload("xcore", lambda: plan.arrived("x"), routes.core)
    plan.payload("g", lambda: cotangent, routes.image)
    plan.payload("gcore", lambda: plan.arrived("g"), routes.core)
    both = lambda name: plan.get(name)

    labels_here = crop_labels.reshape(-1, IMG_TOK)
    labels_there = send(labels_here, routes.core)
    smalls = [piece_a] + [plan.arrived(f"ga{k}z") for k in eye[1:]]

    labels = jnp.where((z & 1) == c, labels_here, labels_there)
    labels = lax.dynamic_index_in_dim(labels, z >> 1, axis=0, keepdims=False)
    row_here = targets(labels, c).reshape(2, HALF)
    row_there = targets(labels, 1 - c).reshape(2, HALF)
    row = lambda t, i: lax.dynamic_slice_in_dim(t, i, 1)
    row_own, row_oth, row_back = row(row_here, c), row(row_here, 1 - c), row(row_there, c)
    vec = jnp.stack(
        [f(t) for t in (norm1_gain, norm1_bias, norm2_gain, norm2_bias, fc2_bias, out_bias, fc2_bias, fc2_bias)]
    )

    low, high, turned = ((ROWS, D), BF), ((ROWS, D), F32), ((D, ROWS), BF)
    flip = [pltpu.VMEM((D, ROWS), BF)]
    whole = [pltpu.VMEM((D, D), BF)]
    block = lambda n: ((4, n, D), BF)

    xs, n1 = plan.run("select", select_body, [low, low], [*both("xcore"), row_own, row_oth, vec], 1.05)

    att = jnp.zeros((ROWS, D), F32)
    qkv, probs, ctx = [], [], []
    for k in eye:
        operands = [n1, wa0] if k == 0 else [order, n1, *both(owner["ga", k])]
        got = plan.run(
            f"attend{k}",
            lambda *refs, k=k: attend_body(k == 0, *refs),
            [((ROWS, 576), BF), ((3, ROWS, 256), BF), ((ROWS, 192), BF), high],
            operands + [smalls[k], att], 3.0, scratch=whole if k else (), hold=-2, alias={-1: 3},
        )
        qkv.append(got[0])
        probs.append(got[1])
        ctx.append(got[2])
        att = got[3]
    middle, n2, n2t = plan.run(
        "middle", middle_body, [high, low, turned], [order, xs, att, vec], 1.15, scratch=flip, hold=3
    )
    gs, gst = plan.run(
        "top", select_top_body, [low, turned], [order, *both("gcore"), row_own, row_oth], 1.4,
        scratch=flip, hold=3,
    )

    parts = {}

    class Sum:
        def __init__(self, kind, slots):
            self.tag, self.kind, self.slots = kind + "".join(map(str, slots)), kind, slots
            plan.payload(self.tag + "far", lambda: self.stack(slice(2, 4)), routes.second)
            plan.payload(self.tag + "near", lambda: self.stack(1, ("far", 1)), routes.first)
            for i, k in enumerate(slots):
                plan.payload(
                    f"{kind}{k}home",
                    lambda i=i: self.add(i, 0, ("far", 0), ("near", Ellipsis)).astype(BF),
                    routes.z[k] if k and kind not in HALVES else None,
                )

        def add(self, i, part, *more):
            keep, core = parts[self.kind, self.slots[i]]
            total = f(keep[part]) + f(core[part])
            for name, place in more:
                total = total + f(plan.arrived(self.tag + name)[i][place])
            return total

        def stack(self, *what):
            return jnp.stack([self.add(i, *what) for i in range(len(self.slots))]).astype(BF)

    for kind in ("f", "a"):
        for slots in GROUPS[kind]:
            Sum(kind, slots)
        if kind in HALVES:
            sent = lambda k, kind=kind: plan.get(f"{kind}{k}home")[0]
            plan.payload(kind + "zone", lambda sent=sent: jnp.stack([sent(1), sent(3)]), routes.z[1])
            plan.payload(
                kind + "ztwo",
                lambda sent=sent, kind=kind: (f(sent(2)) + f(plan.arrived(kind + "zone")[1])).astype(BF),
                routes.z[2],
            )

    def gather_up(tag):
        if tag in HALVES:
            total = f(plan.get(f"{tag}0home")[0]) + f(plan.arrived(tag + "zone")[0])
            total = total + f(plan.arrived(tag + "ztwo"))
        else:
            total = sum(f(plan.arrived(f"{tag}{k}home")) for k in eye)
        for route in routes.group:
            total = total + f(send(total.astype(BF), route))
        return total.astype(BF)

    ffn = gn2 = jnp.zeros((ROWS, D), F32)
    b1_rows = []
    for k in eye:
        hold = [pltpu.VMEM((ROWS, D), BF)] * 2
        if k == 0:
            operands = [n2, gs, n2t, gst, fc1_weight, fc2_weight]
        else:
            operands = [order, n2, gs, n2t, gst, *both(owner["gf", k])]
            hold = hold + whole * 2
        keep, away, brow, ffn, gn2 = plan.run(
            f"hidden{k}",
            lambda *refs, k=k: hidden_body(k == 0, *refs),
            [block(192), block(192), ((1, D), F32), high, high],
            operands + [smalls[k], ffn, gn2], 4.0, scratch=hold, hold=-3, alias={-2: 3, -1: 4},
        )
        parts["f", k] = (keep, send(away, routes.core))
        b1_rows.append(brow)

    rows_out, gm, ga, sums_one = plan.run(
        "turn", turn_body, [low, high, low, ((8, D), F32)], [middle, ffn, gn2, gs, vec], 1.5, hold=4
    )
    plan.payload("outcore", lambda: rows_out, routes.core)

    def unselect(name, rows, there):
        return plan.run(
            name, unselect_body, [((HALF, D), BF)], [row_own, row_back, rows, there], 0.8, hold=2
        )[0]

    plan.payload("out", lambda: unselect("unout", *both("outcore")), routes.image)

    gn1 = jnp.zeros((ROWS, D), F32)
    qkv_rows = [None] * mp
    for k in reversed(eye):
        keep, away, brow, gn1 = plan.run(
            f"back{k}",
            lambda *refs, k=k: attend_back_body(k == 0, *refs),
            [block(96), block(96), ((1, 576), F32), high],
            [order, ga, n1, *([wa0] if k == 0 else both(owner["ga", k])), qkv[k], probs[k], ctx[k], gn1],
            5.0,
            scratch=[
                pltpu.VMEM((ROWS, 192), BF), pltpu.VMEM((ROWS, 576), BF), pltpu.VMEM((D, D), BF),
                *(whole if k else []),
            ],
            hold=0, alias={-1: 3},
        )
        parts["a", k] = (keep, send(away, routes.core))
        qkv_rows[k] = brow
    rows_in, sums = plan.run(
        "last", last_body, [low, ((16, D), F32)],
        [order, xs, gm, gn1, vec, sums_one, *b1_rows, *qkv_rows], 1.45, hold=4,
    )
    plan.payload("incore", lambda: rows_in, routes.core)
    plan.payload("in", lambda: unselect("unin", *both("incore")), routes.image)
    steps = [routes.core, routes.x, routes.y, routes.z[1], routes.z[2], *routes.group]
    plan.payload("s0", lambda: sums, steps[0])
    for i in range(1, len(steps) + 1):
        route = steps[i] if i < len(steps) else None
        plan.payload(f"s{i}", lambda i=i: sum(plan.get(f"s{i - 1}")), route)
    legs("hf", [""], lambda: gather_up("f")[None], 192)
    legs("ha", [""], lambda: gather_up("a")[None], 96)

    fc1_grad, fc2_grad = plan.run(
        "endf", hidden_final_body, [((D, D), F32)] * 2, [order, *both("hfown")], 3.7,
        scratch=[
            pltpu.VMEM((D, D), F32), pltpu.VMEM((D, D), BF), pltpu.VMEM((D, D), F32),
            pltpu.SemaphoreType.DMA((14,)),
        ],
        hold=1, out_far=True,
    )
    qkv_grad, out_grad = plan.run(
        "enda", attend_final_body, [((3, 192, D), F32), ((192, D), F32)], [order, *both("haown")], 2.2,
        scratch=[pltpu.VMEM((D, D), F32), pltpu.SemaphoreType.DMA((4,))], hold=1, out_far=True,
    )
    sums = plan.arrived(f"s{len(steps)}")
    rows_out, rows_in = plan.run(
        "copy", copy_body, [((HALF, D), BF)] * 2, [plan.arrived("out"), plan.arrived("in")], 1.2
    )
    qv_row = lax.dynamic_index_in_dim(sums, 10 + z, axis=0, keepdims=False)
    return (
        rows_out,
        rows_in,
        sums[0],
        sums[1],
        jnp.swapaxes(qkv_grad, 1, 2),
        jnp.stack([qv_row[:192], qv_row[384:576]]),
        out_grad,
        sums[2],
        sums[3],
        sums[4],
        fc1_grad,
        lax.dynamic_index_in_dim(sums, 6 + z, axis=0, keepdims=False),
        fc2_grad,
        sums[5],
    )


def solution(mesh):
    routes = Routes(mesh.shape["dp"], mesh.shape["mp"])
    placed = (
        P(ALL, None), P("dp"), P(), P(), P(None, None, "mp"), P(None, "mp"), P("mp", None), P(),
        P(), P(), P(None, "mp"), P("mp"), P("mp", None), P(), P(ALL, None),
    )
    given = (
        P(ALL, None), P(ALL, None), P(), P(), P(None, None, "mp"), P(None, "mp"), P("mp", None),
        P(), P(), P(), P(None, "mp"), P("mp"), P("mp", None), P(),
    )
    return jax.shard_map(
        lambda *args: local(routes, *args),
        mesh=mesh,
        in_specs=placed,
        out_specs=given,
        check_vma=False,
    )
```

```python
import jax
import jax.numpy as jnp
from jax import lax
from jax.experimental import pallas as pl
from jax.experimental.pallas import tpu as pltpu
from jax.sharding import PartitionSpec as P

HEAD_DIM = 64
IMG_TOK = 690
HALF = 345
BIG = 197
SMALL = 37
BIG_PAD = 208
ROWS = 368
D = 768
BF = jnp.bfloat16
F32 = jnp.float32
ALL = ("dp", "mp")


def nt(a, b):
    return lax.dot_general(a, b, (((1,), (1,)), ((), ())), preferred_element_type=F32)


def tn(a, b):
    return lax.dot_general(a, b, (((0,), (0,)), ((), ())), preferred_element_type=F32)


def nn(a, b):
    return lax.dot_general(a, b, (((1,), (0,)), ((), ())), preferred_element_type=F32)


class Routes:
    def __init__(self, dp, mp):
        self.dp, self.mp = dp, mp
        self.groups = dp // 8

        def table(move):
            pairs = []
            for d in range(dp):
                for z in range(mp):
                    g, y, x, c = d >> 3, (d >> 2) & 1, (d >> 1) & 1, d & 1
                    g2, y2, x2, c2, z2 = move(g, y, x, c, z)
                    pairs.append((d * mp + z, (g2 * 8 + y2 * 4 + x2 * 2 + c2) * mp + z2))
            return pairs

        self.core = table(lambda g, y, x, c, z: (g, y, x, 1 - c, z))
        self.first = table(
            lambda g, y, x, c, z: (g, y, 1 - x, c, z) if c == 0 else (g, 1 - y, x, c, z)
        )
        self.second = table(
            lambda g, y, x, c, z: (g, 1 - y, x, c, z) if c == 0 else (g, y, 1 - x, c, z)
        )
        self.x = table(lambda g, y, x, c, z: (g, y, 1 - x, c, z))
        self.y = table(lambda g, y, x, c, z: (g, 1 - y, x, c, z))
        self.z = [table(lambda g, y, x, c, z, k=k: (g, y, x, c, z ^ k)) for k in range(mp)]
        self.image = table(
            lambda g, y, x, c, z: (g, y, x, 1 - c, z ^ 1) if c != (z & 1) else (g, y, x, c, z)
        )
        self.group = [
            table(lambda g, y, x, c, z, b=b: (g ^ b, y, x, c, z))
            for b in (1 << i for i in range(max(self.groups.bit_length() - 1, 0)))
        ]


def send(value, route):
    return lax.ppermute(value, ALL, route)


def after(value, *others):
    return lax.optimization_barrier((value, *others))[0]


def choose(stack, places):
    return jnp.stack([lax.dynamic_index_in_dim(stack, i, keepdims=False) for i in places])


def norm_stats(values):
    average = jnp.mean(values, axis=-1, keepdims=True)
    centred = values - average
    spread = jnp.mean(centred * centred, axis=-1, keepdims=True)
    scale = lax.rsqrt(spread + 1e-06)
    return centred * scale, scale


def norm_back(hat, scale, gain, grad):
    inner = grad * gain
    a = jnp.mean(inner, axis=-1, keepdims=True)
    b = jnp.mean(inner * hat, axis=-1, keepdims=True)
    return scale * (inner - a - hat * b)


def block_mask(size, small):
    i = lax.broadcasted_iota(jnp.int32, (size, size), 0)
    j = lax.broadcasted_iota(jnp.int32, (size, size), 1)
    if not small:
        return j < BIG
    return (i // SMALL == j // SMALL) & (j < 4 * SMALL)


PARTS = ((0, BIG_PAD, False), (BIG_PAD, ROWS - BIG_PAD, True))


def targets(labels, c):
    crops = jnp.arange(10, dtype=jnp.int32)
    member = labels[:, None] == crops[None, :]
    ahead = (crops[None, :] < crops[:, None]).astype(jnp.int32)
    count = jnp.sum(member.astype(jnp.int32), axis=0)
    big = (count > 100).astype(jnp.int32)
    start = jnp.sum(ahead * count[None, :], axis=1)
    rank_big = jnp.sum(ahead * big[None, :], axis=1)
    rank_small = jnp.sum(ahead * (1 - big)[None, :], axis=1)
    core = jnp.where(big == 1, rank_big, rank_small // 4)
    base = jnp.where(big == 1, 0, BIG_PAD + (rank_small % 4) * SMALL)
    shift = jnp.where(core == c, base - start, -100000)
    place = jnp.arange(labels.shape[0], dtype=jnp.int32)
    row = place + jnp.sum(jnp.where(member, shift[None, :], 0), axis=1)
    return jnp.where(row < 0, -1, row)


def kernel(body, outs, args, us, scratch=(), far=(), alias=None, out_far=False, room=18):
    vmem = pl.BlockSpec(memory_space=pltpu.VMEM)
    smem = pl.BlockSpec(memory_space=pltpu.SMEM)
    return pl.pallas_call(
        body,
        out_shape=tuple(jax.ShapeDtypeStruct(shape, kind) for shape, kind in outs),
        in_specs=[smem if a.ndim == 1 else pl.BlockSpec(memory_space=pl.ANY) if i in far else vmem for i, a in enumerate(args)],
        out_specs=tuple(pl.BlockSpec(memory_space=pl.ANY) if out_far else vmem for _ in outs),
        scratch_shapes=list(scratch),
        input_output_aliases={i % len(args): o for i, o in (alias or {}).items()},
        compiler_params=pltpu.CompilerParams(vmem_limit_bytes=room << 20),
        cost_estimate=pl.CostEstimate(
            flops=int(us * 1.15e9), bytes_accessed=0, transcendentals=0
        ),
    )(*args)


def put_in_order(order, source, out):
    for j in range(8):
        at = pl.multiple_of(order[j] * 96, 96)
        out[96 * j : 96 * j + 96, :] = source[pl.ds(at, 96), :]


def put_back(order, own, oth, out, first=0, size=96):
    for j in range(8):
        at = pl.multiple_of(order[j] * 96, 96)
        part = (own, oth)[j // 4][j % 4, first : first + size, :]
        out[pl.ds(at, size), :] = part.astype(out.dtype)


def piece_body(rows, b1, qv, piece):
    piece[0:96, :] = rows[...]
    row = lax.broadcasted_iota(jnp.int32, (16, D), 0)
    second = jnp.concatenate([qv[0:1, :], qv[1:2, :], qv[0:1, :], qv[1:2, :]], axis=1)
    piece[96:112, :] = jnp.where(row == 0, b1[...].astype(F32), second.astype(F32)).astype(BF)


def copy_body(one, two, first, second):
    first[...] = one[...]
    second[...] = two[...]


def put_together(shape, pieces, arrays):
    def body(*refs):
        out = refs[-1]
        for where, terms in pieces:
            if len(terms) == 1:
                out[where] = refs[terms[0][0]][terms[0][1]]
            else:
                total = refs[terms[0][0]][terms[0][1]].astype(F32)
                for array, place in terms[1:]:
                    total = total + refs[array][place].astype(F32)
                out[where] = total.astype(BF)

    return kernel(body, [(shape, BF)], arrays, 0.5, room=8)[0]


def select_body(own, oth, ro, rt, vec, xs, n1):
    if JOINED:
        own, oth = own.at[0], oth.at[0]
    slots = lax.broadcasted_iota(jnp.int32, (ROWS, HALF), 0)
    pick_own = (slots == ro[...]).astype(F32).astype(BF)
    pick_oth = (slots == rt[...]).astype(F32).astype(BF)
    rows = nn(pick_own, own[...]) + nn(pick_oth, oth[...])
    xs[...] = rows.astype(BF)
    hat, _ = norm_stats(rows)
    normed = hat * vec[0:1, :] + vec[1:2, :]
    n1[...] = normed.astype(BF)


def select_top_body(order, own, oth, ro, rt, gs, gst, flip):
    if JOINED:
        own, oth = own.at[1], oth.at[1]
    slots = lax.broadcasted_iota(jnp.int32, (ROWS, HALF), 0)
    pick_own = (slots == ro[...]).astype(F32).astype(BF)
    pick_oth = (slots == rt[...]).astype(F32).astype(BF)
    grads = (nn(pick_own, own[...]) + nn(pick_oth, oth[...])).astype(BF)
    gs[...] = grads
    flip[...] = grads.T
    put_in_order(order, flip, gst)


def unselect_body(ro, rb, own, oth, out):
    slots = lax.broadcasted_iota(jnp.int32, (ROWS, HALF), 0)
    pick_own = (slots == ro[...]).astype(F32).astype(BF)
    pick_back = (slots == rb[...]).astype(F32).astype(BF)
    out[...] = (tn(pick_own, own[...]) + tn(pick_back, oth[...])).astype(BF)


def heads_of(ref, cut, first):
    return [ref[cut, first + 64 * h : first + 64 * h + 64] for h in range(3)]


def attend_body(assembled, *refs):
    if assembled:
        n1, w, small, add, qkv, probs, ctx, att = refs
    else:
        order, n1, own, oth, small, add, qkv, probs, ctx, att, w = refs
        put_back(order, own, oth, w)
    values = nt(n1[...], w[0:576, :])
    at = small.shape[0] - 15
    shift = small[at : at + 1, 0:384].astype(F32)
    qkv[:, 0:192] = (values[:, 0:192] + shift[:, 0:192]).astype(BF)
    qkv[:, 192:384] = values[:, 192:384].astype(BF)
    qkv[:, 384:576] = (values[:, 384:576] + shift[:, 192:384]).astype(BF)
    for at, size, block in PARTS:
        cut = slice(at, at + size)
        queries, keys, inner = (heads_of(qkv, cut, first) for first in (0, 192, 384))
        mask = block_mask(size, block)
        logits = [jnp.where(mask, nt(q, k) * 0.125, -1e9) for q, k in zip(queries, keys)]
        e = [jnp.exp(t - jnp.max(t, axis=-1, keepdims=True)) for t in logits]
        p = [(t / jnp.sum(t, axis=-1, keepdims=True)).astype(BF) for t in e]
        for h in range(3):
            probs[h, cut, 0:size] = p[h]
        ctx[cut, :] = jnp.concatenate([nn(s, v).astype(BF) for s, v in zip(p, inner)], axis=1)
    att[...] = add[...] + nn(ctx[...], w[576:768, :])


def middle_body(order, xs, att, vec, middle, n2, n2t, flip):
    mid = xs[...].astype(F32) + att[...] + vec[5:6, :]
    middle[...] = mid
    hat, _ = norm_stats(mid)
    normed = (hat * vec[2:3, :] + vec[3:4, :]).astype(BF)
    n2[...] = normed
    flip[...] = normed.T
    put_in_order(order, flip, n2t)


def hidden_body(assembled, *refs):
    if assembled:
        n2, gs, n2t, gst, w1, w2, small, out_in, gn_in, *refs = refs
        keep, away, brow, out, gn, act, gb = refs
    else:
        order, n2, gs, n2t, gst, own, oth, small, out_in, gn_in, *refs = refs
        keep, away, brow, out, gn, act, gb, w1, w2 = refs
        put_back(order, own, oth, w1)
        put_back(order, own, oth, w2, 96)
    at = small.shape[0] - 16
    shift = small[at : at + 1, :].astype(F32)
    for at in range(0, D, 256):
        cut = slice(at, at + 256)
        before = nn(n2[...], w1[:, cut]) + shift[:, cut]
        cdf = 0.5 + 0.5 * lax.erf(before * (0.5**0.5))
        act[:, cut] = (before * cdf).astype(BF)
        slope = cdf + before * jnp.exp(-0.5 * before * before) * 0.3989422804014327
        grad = (nt(gs[...], w2[cut, :]) * slope).astype(BF)
        gb[:, cut] = grad
        brow[:, cut] = jnp.sum(grad.astype(F32), axis=0, keepdims=True)
    out[...] = out_in[...] + nn(act[...], w2[...])
    gn[...] = gn_in[...] + nt(gb[...], w1[...])
    for half, target in ((0, keep), (384, away)):
        first = nn(n2t[half : half + 384, :], gb[...]).astype(BF)
        second = nn(gst[half : half + 384, :], act[...]).astype(BF)
        for j in range(4):
            target[j, 0:96, :] = first[96 * j : 96 * j + 96]
            target[j, 96:192, :] = second[96 * j : 96 * j + 96]


def turn_body(middle, ffn, gn2, gs, vec, rows_out, gm, ga, sums):
    mid = middle[...]
    rows_out[...] = (mid + ffn[...] + vec[6:7, :]).astype(BF)
    hat, scale = norm_stats(mid)
    grad = gn2[...]
    top = gs[...].astype(F32)
    total = top + norm_back(hat, scale, vec[2:3, :], grad)
    gm[...] = total
    low = total.astype(BF)
    ga[...] = low
    sums[...] = jnp.zeros(sums.shape, F32)
    sums[0:1, :] = jnp.sum(low.astype(F32), axis=0, keepdims=True)
    sums[1:2, :] = jnp.sum(grad * hat, axis=0, keepdims=True)
    sums[2:3, :] = jnp.sum(grad, axis=0, keepdims=True)
    sums[3:4, :] = jnp.sum(top, axis=0, keepdims=True)


def attend_back_body(assembled, *refs):
    order, ga, n1, *refs = refs
    if assembled:
        w, qkv, probs, ctx, gn_in, keep, away, brow, gn, gc, dqkv, full = refs
    else:
        own, oth, qkv, probs, ctx, gn_in, keep, away, brow, gn, gc, dqkv, full, w = refs
        put_back(order, own, oth, w)
    gc[...] = nt(ga[...], w[576:768, :]).astype(BF)
    for at, size, _ in PARTS:
        cut = slice(at, at + size)
        queries, keys, inner = (heads_of(qkv, cut, first) for first in (0, 192, 384))
        tops = heads_of(gc, cut, 0)
        low = [probs[h, cut, 0:size] for h in range(3)]
        p = [t.astype(F32) for t in low]
        gp = [nt(g, v) for g, v in zip(tops, inner)]
        ds = [
            (a * (b - jnp.sum(a * b, axis=-1, keepdims=True)) * 0.125).astype(BF)
            for a, b in zip(p, gp)
        ]
        dv = [tn(a, g).astype(BF) for a, g in zip(low, tops)]
        dq = [nn(a, k).astype(BF) for a, k in zip(ds, keys)]
        dk = [tn(a, q).astype(BF) for a, q in zip(ds, queries)]
        dqkv[cut, :] = jnp.concatenate(dq + dk + dv, axis=1)
    grads = dqkv[...]
    brow[...] = jnp.sum(grads.astype(F32), axis=0, keepdims=True)
    full[0:576, :] = tn(grads, n1[...]).astype(BF)
    full[576:768, :] = tn(ctx[...], ga[...]).astype(BF)
    for j in range(8):
        at = pl.multiple_of(order[j] * 96, 96)
        (keep, away)[j // 4][j % 4, :, :] = full[pl.ds(at, 96), :]
    gn[...] = gn_in[...] + nn(grads, w[0:576, :])


def last_body(order, xs, gm, gn1, vec, one, *refs):
    b1_rows, qkv_rows, rows_out, sums = refs[:4], refs[4:8], refs[8], refs[9]
    hat, scale = norm_stats(xs[...].astype(F32))
    grad = gn1[...]
    rows_out[...] = (gm[...] + norm_back(hat, scale, vec[0:1, :], grad)).astype(BF)
    sums[...] = jnp.zeros(sums.shape, F32)
    sums[0:1, :] = jnp.sum(grad * hat, axis=0, keepdims=True)
    sums[1:2, :] = jnp.sum(grad, axis=0, keepdims=True)
    sums[2:6, :] = one[0:4, :]
    for k in range(4):
        shard = order[8] ^ k
        sums[pl.ds(6 + shard, 1), :] = b1_rows[k][...]
        sums[pl.ds(10 + shard, 1), 0:576] = qkv_rows[k][...]


def hidden_final_body(order, own, oth, first, second, flat, flip, turned, sems):
    copies = []
    for j in range(8):
        at = pl.multiple_of(order[j] * 96, 96)
        part = (own, oth)[j // 4].at[j % 4]
        flat[96 * j : 96 * j + 96, :] = part[0:96, :].astype(F32)
        flip[pl.ds(at, 96), :] = part[96:192, :]
        copies.append(
            pltpu.make_async_copy(flat.at[pl.ds(96 * j, 96)], first.at[pl.ds(at, 96)], sems.at[j])
        )
        copies[-1].start()
    for i in range(6):
        cut = slice(128 * i, 128 * i + 128)
        turned[cut, :] = flip[:, cut].T.astype(F32)
        rows = pl.ds(128 * i, 128)
        copies.append(pltpu.make_async_copy(turned.at[rows], second.at[rows], sems.at[8 + i]))
        copies[-1].start()
    for copy in copies:
        copy.wait()


def attend_final_body(order, own, oth, qkv, out, full, sems):
    put_back(order, own, oth, full)
    copies = [
        pltpu.make_async_copy(full.at[pl.ds(192 * i, 192)], qkv.at[i] if i < 3 else out, sems.at[i])
        for i in range(4)
    ]
    for copy in copies:
        copy.start()
    for copy in copies:
        copy.wait()


GROUPS = {
    "ga": ((1,), (2, 3)),
    "gf": ((1,), (2,), (3,)),
    "f": ((0,), (1,), (2,), (3,)),
    "a": ((3,), (2,), (1,), (0,)),
}
JOINED = False
HALVES = ("f", "a")
COSTS = {
    "enda": 0.017,
    "attend2": 3.92,
    "hidden3": 8.0,
    "hidden0": 0.35,
    "back1": 0.8,
    "unout": 0.1,
    "unin": 8.0,
    "attend3": 8.0,
    "top": 0.7,
    "attend0": 0.07,
    "back2": 0.062,
    "copy": 0.025,
    "select": 4.0,
    "back0": 0.05,
    "hidden2": 0.25,
    "attend1": 8.0,
    "turn": 0.1,
    "hidden1": 2.0,
}
BEFORE = {
    "a3home": "back0",
    "xcore": "hidden0",
    "f1near": "back2",
    "f3near": "unout",
    "f1far": "turn",
    "fzone": "last",
    "ga1one": "top",
    "a3far": "back1",
    "f2far": "back2",
    "gf1z": "last",
    "f0near": "back3",
    "a2far": "back1",
    "f0home": "enda",
    "ga2two": "enda",
    "out": "select",
    "gcore": "unin",
    "outcore": "back1",
    "ga23two": "attend0",
    "a2home": "back0",
    "gf1two": "last",
    "gf2own2": "unin",
    "a1near": "enda",
    "f2home": "unout",
    "s3": "attend2",
    "f0far": "hidden2",
    "x": "attend1",
    "ga2own2": "back2",
    "f3far": "back2",
    "f2near": "back1",
    "s5": "unin",
}
AFTER = {
    "ga3z": "hidden1",
    "g": "attend2",
    "f2home": "endf",
    "ga3two": "back0",
    "gf2one": "endf",
    "haown": "top",
    "gf1own1": "unout",
    "gf3two": "back1",
    "a3far": "hidden0",
    "a0far": "unout",
    "f2far": "attend3",
    "ga1own1": "unout",
    "gf3one": "attend1",
    "ga1one": "attend3",
    "f3far": "unin",
    "ga2z": "attend0",
    "haone": "s3",
    "gf1one": "select",
    "a0near": "last",
    "azone": "s1",
    "aztwo": "s2",
    "hatwo": "s4",
    "hfone": "gf2two",
    "f0near": "back0",
}


class Plan:
    def __init__(self):
        self.makers, self.values, self.outputs = {}, {}, {}

    def payload(self, name, make, route):
        self.makers[name] = (make, route)

    def get(self, name):
        if name not in self.values:
            make, route = self.makers[name]
            value = make()
            late = AFTER.get(name)
            if late in self.outputs:
                value = after(value, self.outputs[late])
            elif late in self.makers:
                value = after(value, self.get(late)[0])
            self.values[name] = (value, value if route is None else send(value, route))
        return self.values[name]

    def arrived(self, name):
        return self.get(name)[1]

    def run(self, name, body, outs, args, us, scratch=(), hold=0, alias=None, out_far=False):
        gates = []
        for payload, late in BEFORE.items():
            if late == name:
                try:
                    gates.append(self.get(payload)[0])
                except KeyError:
                    pass
        args = list(args)
        if gates:
            args[hold] = after(args[hold], *gates)
        got = kernel(body, outs, args, us * COSTS.get(name, 1.0), scratch, (), alias, out_far)
        self.outputs[name] = got[-1]
        return got


def local(routes, *args):
    (
        inputs, crop_labels, norm1_gain, norm1_bias, qkv_weight, qv_bias, out_weight, out_bias,
        norm2_gain, norm2_bias, fc1_weight, fc1_bias, fc2_weight, fc2_bias, cotangent,
    ) = args
    dp, z = lax.axis_index("dp"), lax.axis_index("mp")
    c, x, y = dp & 1, (dp >> 1) & 1, (dp >> 2) & 1
    quarter = y * 2 + x
    mp = routes.mp
    eye = list(range(mp))
    f = lambda t: t.astype(F32)
    plan = Plan()

    def order_of(colour):
        near = jnp.where(colour == 0, 1, 2)
        far = 3 - near
        return [colour * 4 + (quarter ^ d) for d in (jnp.zeros_like(near), near, far, far + near)]

    order = jnp.stack(order_of(c) + order_of(1 - c) + [z]).astype(jnp.int32)

    start = (c * 4 + quarter) * 96
    heads_w = [jnp.swapaxes(qkv_weight, 1, 2).reshape(-1, D), out_weight]
    rows_a = lax.dynamic_slice_in_dim(jnp.concatenate(heads_w), start, 96)
    (piece_a,) = kernel(
        piece_body, [((112, D), BF)], [rows_a, fc1_bias[None], qv_bias], 0.3, room=8
    )
    wa0 = put_together(
        (D, D),
        [((slice(0, 576),), [(0, (Ellipsis,))]), ((slice(576, D),), [(1, (Ellipsis,))])],
        heads_w,
    )
    piece_f = put_together(
        (192, D),
        [((slice(96 * i, 96 * i + 96),), [(i, (Ellipsis,))]) for i in range(2)],
        [lax.dynamic_slice_in_dim(t, start, 96) for t in (fc1_weight, fc2_weight)],
    )

    owner = {}

    def legs(tag, slots, first, rows):
        def own(i):
            whole = slice(None)
            return put_together(
                (4, rows, D),
                [((slice(2 * j, 2 * j + 2),), [(j, (whole, i))]) for j in range(2)],
                plan.get(tag + "two"),
            )

        plan.payload(tag + "one", first, routes.first)
        plan.payload(
            tag + "two",
            lambda: put_together(
                (2, len(slots), rows, D),
                [((j,), [(j, (slice(None), slice(0, rows)))]) for j in range(2)],
                plan.get(tag + "one"),
            ),
            routes.second,
        )
        for i, k in enumerate(slots):
            owner[tag[:2], k] = f"{tag}own{k}"
            plan.payload(f"{tag}own{k}", lambda i=i: own(i), routes.core)

    for kind, piece, rows in (("ga", piece_a, 96), ("gf", piece_f, 192)):
        for k in eye[1:]:
            plan.payload(f"{kind}{k}z", lambda piece=piece: piece, routes.z[k])
        for slots in GROUPS[kind]:
            legs(
                kind + "".join(map(str, slots)), slots,
                lambda kind=kind, slots=slots: jnp.stack([plan.arrived(f"{kind}{k}z") for k in slots]),
                rows,
            )
    def rows_in_one():
        places = [((j,), [(j, (Ellipsis,))]) for j in range(2)]
        return put_together((2, HALF, D), places, [inputs, cotangent])

    plan.payload("x", rows_in_one if JOINED else lambda: inputs, routes.image)
    plan.payload("xcore", lambda: plan.arrived("x"), routes.core)
    plan.payload("g", lambda: cotangent, routes.image)
    plan.payload("gcore", lambda: plan.arrived("g"), routes.core)
    both = lambda name: plan.get(name)

    labels_here = crop_labels.reshape(-1, IMG_TOK)
    labels_there = send(labels_here, routes.core)
    smalls = [piece_a] + [plan.arrived(f"ga{k}z") for k in eye[1:]]

    labels = jnp.where((z & 1) == c, labels_here, labels_there)
    labels = lax.dynamic_index_in_dim(labels, z >> 1, axis=0, keepdims=False)
    row_here = targets(labels, c).reshape(2, HALF)
    row_there = targets(labels, 1 - c).reshape(2, HALF)
    row = lambda t, i: lax.dynamic_slice_in_dim(t, i, 1)
    row_own, row_oth, row_back = row(row_here, c), row(row_here, 1 - c), row(row_there, c)
    vec = jnp.stack(
        [f(t) for t in (norm1_gain, norm1_bias, norm2_gain, norm2_bias, fc2_bias, out_bias, fc2_bias, fc2_bias)]
    )

    low, high, turned = ((ROWS, D), BF), ((ROWS, D), F32), ((D, ROWS), BF)
    flip = [pltpu.VMEM((D, ROWS), BF)]
    whole = [pltpu.VMEM((D, D), BF)]
    block = lambda n: ((4, n, D), BF)

    xs, n1 = plan.run("select", select_body, [low, low], [*both("xcore"), row_own, row_oth, vec], 1.05)

    att = jnp.zeros((ROWS, D), F32)
    qkv, probs, ctx = [], [], []
    for k in eye:
        operands = [n1, wa0] if k == 0 else [order, n1, *both(owner["ga", k])]
        got = plan.run(
            f"attend{k}",
            lambda *refs, k=k: attend_body(k == 0, *refs),
            [((ROWS, 576), BF), ((3, ROWS, 256), BF), ((ROWS, 192), BF), high],
            operands + [smalls[k], att], 3.0, scratch=whole if k else (), hold=-2, alias={-1: 3},
        )
        qkv.append(got[0])
        probs.append(got[1])
        ctx.append(got[2])
        att = got[3]
    middle, n2, n2t = plan.run(
        "middle", middle_body, [high, low, turned], [order, xs, att, vec], 1.15, scratch=flip, hold=3
    )
    gs, gst = plan.run(
        "top", select_top_body, [low, turned], [order, *both("xcore" if JOINED else "gcore"), row_own, row_oth], 1.4,
        scratch=flip, hold=3,
    )

    parts = {}

    class Sum:
        def __init__(self, kind, slots):
            self.tag, self.kind, self.slots = kind + "".join(map(str, slots)), kind, slots
            plan.payload(self.tag + "far", lambda: self.gather(slice(2, 4)), routes.second)
            plan.payload(self.tag + "near", lambda: self.gather(1, ("far", (1,)), ), routes.first)
            for i, k in enumerate(slots):
                plan.payload(
                    f"{kind}{k}home",
                    lambda i=i: self.one(i),
                    routes.z[k] if k and kind not in HALVES else None,
                )

        def gather(self, part, *more):
            arrays = [t for k in self.slots for t in parts[self.kind, k]]
            arrays += [plan.arrived(self.tag + name) for name, _ in more]
            at = 2 * len(self.slots)
            rows = {"f": 192, "a": 96}[self.kind]
            pieces = [
                ((i,), [(2 * i, (part,)), (2 * i + 1, (part,))] + [(at + n, (i, *place)) for n, (_, place) in enumerate(more)])
                for i in range(len(self.slots))
            ]
            depth = (2,) if isinstance(part, slice) else ()
            return put_together((len(self.slots), *depth, rows, D), pieces, arrays)

        def one(self, i):
            keep, core = parts[self.kind, self.slots[i]]
            rows = {"f": 192, "a": 96}[self.kind]
            arrays = [keep, core, plan.arrived(self.tag + "far"), plan.arrived(self.tag + "near")]
            return put_together(
                (rows, D), [((Ellipsis,), [(0, (0,)), (1, (0,)), (2, (i, 0)), (3, (i,))])], arrays
            )

    for kind in ("f", "a"):
        for slots in GROUPS[kind]:
            Sum(kind, slots)
        if kind in HALVES:
            sent = lambda k, kind=kind: plan.get(f"{kind}{k}home")[0]
            plan.payload(kind + "zone", lambda sent=sent: jnp.stack([sent(1), sent(3)]), routes.z[1])
            plan.payload(
                kind + "ztwo",
                lambda sent=sent, kind=kind: (f(sent(2)) + f(plan.arrived(kind + "zone")[1])).astype(BF),
                routes.z[2],
            )

    def gather_up(tag):
        rows = {"f": 192, "a": 96}[tag]
        if tag in HALVES:
            arrays = [plan.get(f"{tag}0home")[0], plan.arrived(tag + "zone"), plan.arrived(tag + "ztwo")]
            places = [(0, (Ellipsis,)), (1, (0,)), (2, (Ellipsis,))]
        else:
            arrays = [plan.arrived(f"{tag}{k}home") for k in eye]
            places = [(k, (Ellipsis,)) for k in eye]
        total = put_together((1, rows, D), [((0,), places)], arrays)
        if not routes.group:
            return total
        total = f(total)
        for route in routes.group:
            total = total + f(send(total.astype(BF), route))
        return total.astype(BF)

    ffn = gn2 = jnp.zeros((ROWS, D), F32)
    b1_rows = []
    for k in eye:
        hold = [pltpu.VMEM((ROWS, D), BF)] * 2
        if k == 0:
            operands = [n2, gs, n2t, gst, fc1_weight, fc2_weight]
        else:
            operands = [order, n2, gs, n2t, gst, *both(owner["gf", k])]
            hold = hold + whole * 2
        keep, away, brow, ffn, gn2 = plan.run(
            f"hidden{k}",
            lambda *refs, k=k: hidden_body(k == 0, *refs),
            [block(192), block(192), ((1, D), F32), high, high],
            operands + [smalls[k], ffn, gn2], 4.0, scratch=hold, hold=-3, alias={-2: 3, -1: 4},
        )
        parts["f", k] = (keep, send(away, routes.core))
        b1_rows.append(brow)

    rows_out, gm, ga, sums_one = plan.run(
        "turn", turn_body, [low, high, low, ((8, D), F32)], [middle, ffn, gn2, gs, vec], 1.5, hold=4
    )
    plan.payload("outcore", lambda: rows_out, routes.core)

    def unselect(name, rows, there):
        return plan.run(
            name, unselect_body, [((HALF, D), BF)], [row_own, row_back, rows, there], 0.8, hold=2
        )[0]

    plan.payload("out", lambda: unselect("unout", *both("outcore")), routes.image)

    gn1 = jnp.zeros((ROWS, D), F32)
    qkv_rows = [None] * mp
    for k in reversed(eye):
        keep, away, brow, gn1 = plan.run(
            f"back{k}",
            lambda *refs, k=k: attend_back_body(k == 0, *refs),
            [block(96), block(96), ((1, 576), F32), high],
            [order, ga, n1, *([wa0] if k == 0 else both(owner["ga", k])), qkv[k], probs[k], ctx[k], gn1],
            5.0,
            scratch=[
                pltpu.VMEM((ROWS, 192), BF), pltpu.VMEM((ROWS, 576), BF), pltpu.VMEM((D, D), BF),
                *(whole if k else []),
            ],
            hold=0, alias={-1: 3},
        )
        parts["a", k] = (keep, send(away, routes.core))
        qkv_rows[k] = brow
    rows_in, sums = plan.run(
        "last", last_body, [low, ((16, D), F32)],
        [order, xs, gm, gn1, vec, sums_one, *b1_rows, *qkv_rows], 1.45, hold=4,
    )
    plan.payload("incore", lambda: rows_in, routes.core)
    plan.payload("in", lambda: unselect("unin", *both("incore")), routes.image)
    steps = [routes.core, routes.x, routes.y, routes.z[1], routes.z[2], *routes.group]
    plan.payload("s0", lambda: sums, steps[0])
    for i in range(1, len(steps) + 1):
        route = steps[i] if i < len(steps) else None
        plan.payload(f"s{i}", lambda i=i: sum(plan.get(f"s{i - 1}")), route)
    legs("hf", [""], lambda: gather_up("f"), 192)
    legs("ha", [""], lambda: gather_up("a"), 96)

    fc1_grad, fc2_grad = plan.run(
        "endf", hidden_final_body, [((D, D), F32)] * 2, [order, *both("hfown")], 3.7,
        scratch=[
            pltpu.VMEM((D, D), F32), pltpu.VMEM((D, D), BF), pltpu.VMEM((D, D), F32),
            pltpu.SemaphoreType.DMA((14,)),
        ],
        hold=1, out_far=True,
    )
    qkv_grad, out_grad = plan.run(
        "enda", attend_final_body, [((3, 192, D), F32), ((192, D), F32)], [order, *both("haown")], 2.2,
        scratch=[pltpu.VMEM((D, D), F32), pltpu.SemaphoreType.DMA((4,))], hold=1, out_far=True,
    )
    sums = plan.arrived(f"s{len(steps)}")
    rows_out, rows_in = plan.run(
        "copy", copy_body, [((HALF, D), BF)] * 2, [plan.arrived("out"), plan.arrived("in")], 1.2
    )
    qv_row = lax.dynamic_index_in_dim(sums, 10 + z, axis=0, keepdims=False)
    return (
        rows_out,
        rows_in,
        sums[0],
        sums[1],
        jnp.swapaxes(qkv_grad, 1, 2),
        jnp.stack([qv_row[:192], qv_row[384:576]]),
        out_grad,
        sums[2],
        sums[3],
        sums[4],
        fc1_grad,
        lax.dynamic_index_in_dim(sums, 6 + z, axis=0, keepdims=False),
        fc2_grad,
        sums[5],
    )


def solution(mesh):
    routes = Routes(mesh.shape["dp"], mesh.shape["mp"])
    placed = (
        P(ALL, None), P("dp"), P(), P(), P(None, None, "mp"), P(None, "mp"), P("mp", None), P(),
        P(), P(), P(None, "mp"), P("mp"), P("mp", None), P(), P(ALL, None),
    )
    given = (
        P(ALL, None), P(ALL, None), P(), P(), P(None, None, "mp"), P(None, "mp"), P("mp", None),
        P(), P(), P(), P(None, "mp"), P("mp"), P("mp", None), P(),
    )
    return jax.shard_map(
        lambda *args: local(routes, *args),
        mesh=mesh,
        in_specs=placed,
        out_specs=given,
        check_vma=False,
    )
```

```python
import jax
import jax.numpy as jnp
from jax import lax
from jax.experimental import pallas as pl
from jax.experimental.pallas import tpu as pltpu
from jax.sharding import PartitionSpec as P

HEAD_DIM = 64
IMG_TOK = 690
HALF = 345
BIG = 197
SMALL = 37
BIG_PAD = 208
ROWS = 368
D = 768
BF = jnp.bfloat16
F32 = jnp.float32
ALL = ("dp", "mp")


def nt(a, b):
    return lax.dot_general(a, b, (((1,), (1,)), ((), ())), preferred_element_type=F32)


def tn(a, b):
    return lax.dot_general(a, b, (((0,), (0,)), ((), ())), preferred_element_type=F32)


def nn(a, b):
    return lax.dot_general(a, b, (((1,), (0,)), ((), ())), preferred_element_type=F32)


class Routes:
    def __init__(self, dp, mp):
        self.dp, self.mp = dp, mp
        self.groups = dp // 8

        def table(move):
            pairs = []
            for d in range(dp):
                for z in range(mp):
                    g, y, x, c = d >> 3, (d >> 2) & 1, (d >> 1) & 1, d & 1
                    g2, y2, x2, c2, z2 = move(g, y, x, c, z)
                    pairs.append((d * mp + z, (g2 * 8 + y2 * 4 + x2 * 2 + c2) * mp + z2))
            return pairs

        self.core = table(lambda g, y, x, c, z: (g, y, x, 1 - c, z))
        self.first = table(
            lambda g, y, x, c, z: (g, y, 1 - x, c, z) if c == 0 else (g, 1 - y, x, c, z)
        )
        self.second = table(
            lambda g, y, x, c, z: (g, 1 - y, x, c, z) if c == 0 else (g, y, 1 - x, c, z)
        )
        self.x = table(lambda g, y, x, c, z: (g, y, 1 - x, c, z))
        self.y = table(lambda g, y, x, c, z: (g, 1 - y, x, c, z))
        self.z = [table(lambda g, y, x, c, z, k=k: (g, y, x, c, z ^ k)) for k in range(mp)]
        self.image = table(
            lambda g, y, x, c, z: (g, y, x, 1 - c, z ^ 1) if c != (z & 1) else (g, y, x, c, z)
        )
        self.group = [
            table(lambda g, y, x, c, z, b=b: (g ^ b, y, x, c, z))
            for b in (1 << i for i in range(max(self.groups.bit_length() - 1, 0)))
        ]


def send(value, route):
    return lax.ppermute(value, ALL, route)


def after(value, *others):
    return lax.optimization_barrier((value, *others))[0]


def choose(stack, places):
    return jnp.stack([lax.dynamic_index_in_dim(stack, i, keepdims=False) for i in places])


def norm_stats(values):
    average = jnp.mean(values, axis=-1, keepdims=True)
    centred = values - average
    spread = jnp.mean(centred * centred, axis=-1, keepdims=True)
    scale = lax.rsqrt(spread + 1e-06)
    return centred * scale, scale


def norm_back(hat, scale, gain, grad):
    inner = grad * gain
    a = jnp.mean(inner, axis=-1, keepdims=True)
    b = jnp.mean(inner * hat, axis=-1, keepdims=True)
    return scale * (inner - a - hat * b)


def block_mask(size, small):
    i = lax.broadcasted_iota(jnp.int32, (size, size), 0)
    j = lax.broadcasted_iota(jnp.int32, (size, size), 1)
    if not small:
        return j < BIG
    return (i // SMALL == j // SMALL) & (j < 4 * SMALL)


PARTS = ((0, BIG_PAD, False), (BIG_PAD, ROWS - BIG_PAD, True))


def targets(labels, c):
    crops = jnp.arange(10, dtype=jnp.int32)
    member = labels[:, None] == crops[None, :]
    ahead = (crops[None, :] < crops[:, None]).astype(jnp.int32)
    count = jnp.sum(member.astype(jnp.int32), axis=0)
    big = (count > 100).astype(jnp.int32)
    start = jnp.sum(ahead * count[None, :], axis=1)
    rank_big = jnp.sum(ahead * big[None, :], axis=1)
    rank_small = jnp.sum(ahead * (1 - big)[None, :], axis=1)
    core = jnp.where(big == 1, rank_big, rank_small // 4)
    base = jnp.where(big == 1, 0, BIG_PAD + (rank_small % 4) * SMALL)
    shift = jnp.where(core == c, base - start, -100000)
    place = jnp.arange(labels.shape[0], dtype=jnp.int32)
    row = place + jnp.sum(jnp.where(member, shift[None, :], 0), axis=1)
    return jnp.where(row < 0, -1, row)


def kernel(body, outs, args, us, scratch=(), far=(), alias=None, out_far=False, room=18):
    vmem = pl.BlockSpec(memory_space=pltpu.VMEM)
    smem = pl.BlockSpec(memory_space=pltpu.SMEM)
    return pl.pallas_call(
        body,
        out_shape=tuple(jax.ShapeDtypeStruct(shape, kind) for shape, kind in outs),
        in_specs=[smem if a.ndim == 1 else pl.BlockSpec(memory_space=pl.ANY) if i in far else vmem for i, a in enumerate(args)],
        out_specs=tuple(pl.BlockSpec(memory_space=pl.ANY) if out_far else vmem for _ in outs),
        scratch_shapes=list(scratch),
        input_output_aliases={i % len(args): o for i, o in (alias or {}).items()},
        compiler_params=pltpu.CompilerParams(vmem_limit_bytes=room << 20),
        cost_estimate=pl.CostEstimate(
            flops=int(us * 1.15e9), bytes_accessed=0, transcendentals=0
        ),
    )(*args)


def put_in_order(order, source, out):
    for j in range(8):
        at = pl.multiple_of(order[j] * 96, 96)
        out[96 * j : 96 * j + 96, :] = source[pl.ds(at, 96), :]


def put_back(order, own, oth, out, first=0, size=96):
    for j in range(8):
        at = pl.multiple_of(order[j] * 96, 96)
        part = (own, oth)[j // 4][j % 4, first : first + size, :]
        out[pl.ds(at, size), :] = part.astype(out.dtype)


def piece_body(rows, b1, qv, piece):
    piece[0:96, :] = rows[...]
    row = lax.broadcasted_iota(jnp.int32, (16, D), 0)
    second = jnp.concatenate([qv[0:1, :], qv[1:2, :], qv[0:1, :], qv[1:2, :]], axis=1)
    piece[96:112, :] = jnp.where(row == 0, b1[...].astype(F32), second.astype(F32)).astype(BF)


def copy_body(one, two, first, second):
    first[...] = one[...]
    second[...] = two[...]


def put_together(shape, pieces, arrays):
    def body(*refs):
        out = refs[-1]
        for where, terms in pieces:
            if len(terms) == 1:
                out[where] = refs[terms[0][0]][terms[0][1]]
            else:
                total = refs[terms[0][0]][terms[0][1]].astype(F32)
                for array, place in terms[1:]:
                    total = total + refs[array][place].astype(F32)
                out[where] = total.astype(BF)

    return kernel(body, [(shape, BF)], arrays, 0.5, room=8)[0]


def select_body(own, oth, ro, rt, vec, xs, n1):
    if JOINED:
        own, oth = own.at[0], oth.at[0]
    slots = lax.broadcasted_iota(jnp.int32, (ROWS, HALF), 0)
    pick_own = (slots == ro[...]).astype(F32).astype(BF)
    pick_oth = (slots == rt[...]).astype(F32).astype(BF)
    rows = nn(pick_own, own[...]) + nn(pick_oth, oth[...])
    xs[...] = rows.astype(BF)
    hat, _ = norm_stats(rows)
    normed = hat * vec[0:1, :] + vec[1:2, :]
    n1[...] = normed.astype(BF)


def select_top_body(order, own, oth, ro, rt, gs, gst, flip):
    if JOINED:
        own, oth = own.at[1], oth.at[1]
    slots = lax.broadcasted_iota(jnp.int32, (ROWS, HALF), 0)
    pick_own = (slots == ro[...]).astype(F32).astype(BF)
    pick_oth = (slots == rt[...]).astype(F32).astype(BF)
    grads = (nn(pick_own, own[...]) + nn(pick_oth, oth[...])).astype(BF)
    gs[...] = grads
    flip[...] = grads.T
    put_in_order(order, flip, gst)


def unselect_body(ro, rb, own, oth, out):
    slots = lax.broadcasted_iota(jnp.int32, (ROWS, HALF), 0)
    pick_own = (slots == ro[...]).astype(F32).astype(BF)
    pick_back = (slots == rb[...]).astype(F32).astype(BF)
    out[...] = (tn(pick_own, own[...]) + tn(pick_back, oth[...])).astype(BF)


def heads_of(ref, cut, first):
    return [ref[cut, first + 64 * h : first + 64 * h + 64] for h in range(3)]


def attend_body(assembled, *refs):
    if assembled:
        n1, w, small, add, qkv, probs, ctx, att = refs
    else:
        order, n1, own, oth, small, add, qkv, probs, ctx, att, w = refs
        put_back(order, own, oth, w)
    values = nt(n1[...], w[0:576, :])
    at = small.shape[0] - 15
    shift = small[at : at + 1, 0:384].astype(F32)
    qkv[:, 0:192] = (values[:, 0:192] + shift[:, 0:192]).astype(BF)
    qkv[:, 192:384] = values[:, 192:384].astype(BF)
    qkv[:, 384:576] = (values[:, 384:576] + shift[:, 192:384]).astype(BF)
    for at, size, block in PARTS:
        cut = slice(at, at + size)
        queries, keys, inner = (heads_of(qkv, cut, first) for first in (0, 192, 384))
        mask = block_mask(size, block)
        logits = [jnp.where(mask, nt(q, k) * 0.125, -1e9) for q, k in zip(queries, keys)]
        e = [jnp.exp(t - jnp.max(t, axis=-1, keepdims=True)) for t in logits]
        p = [(t / jnp.sum(t, axis=-1, keepdims=True)).astype(BF) for t in e]
        for h in range(3):
            probs[h, cut, 0:size] = p[h]
        ctx[cut, :] = jnp.concatenate([nn(s, v).astype(BF) for s, v in zip(p, inner)], axis=1)
    att[...] = add[...] + nn(ctx[...], w[576:768, :])


def middle_body(order, xs, att, vec, middle, n2, n2t, flip):
    mid = xs[...].astype(F32) + att[...] + vec[5:6, :]
    middle[...] = mid
    hat, _ = norm_stats(mid)
    normed = (hat * vec[2:3, :] + vec[3:4, :]).astype(BF)
    n2[...] = normed
    flip[...] = normed.T
    put_in_order(order, flip, n2t)


def hidden_body(assembled, *refs):
    if assembled:
        n2, gs, n2t, gst, w1, w2, small, out_in, gn_in, *refs = refs
        keep, away, brow, out, gn, act, gb = refs
    else:
        order, n2, gs, n2t, gst, own, oth, small, out_in, gn_in, *refs = refs
        keep, away, brow, out, gn, act, gb, w1, w2 = refs
        put_back(order, own, oth, w1)
        put_back(order, own, oth, w2, 96)
    at = small.shape[0] - 16
    shift = small[at : at + 1, :].astype(F32)
    for at in range(0, D, 256):
        cut = slice(at, at + 256)
        before = nn(n2[...], w1[:, cut]) + shift[:, cut]
        cdf = 0.5 + 0.5 * lax.erf(before * (0.5**0.5))
        act[:, cut] = (before * cdf).astype(BF)
        slope = cdf + before * jnp.exp(-0.5 * before * before) * 0.3989422804014327
        grad = (nt(gs[...], w2[cut, :]) * slope).astype(BF)
        gb[:, cut] = grad
        brow[:, cut] = jnp.sum(grad.astype(F32), axis=0, keepdims=True)
    out[...] = out_in[...] + nn(act[...], w2[...])
    gn[...] = gn_in[...] + nt(gb[...], w1[...])
    for half, target in ((0, keep), (384, away)):
        first = nn(n2t[half : half + 384, :], gb[...]).astype(BF)
        second = nn(gst[half : half + 384, :], act[...]).astype(BF)
        for j in range(4):
            target[j, 0:96, :] = first[96 * j : 96 * j + 96]
            target[j, 96:192, :] = second[96 * j : 96 * j + 96]


def turn_body(middle, ffn, gn2, gs, vec, rows_out, gm, ga, sums):
    mid = middle[...]
    rows_out[...] = (mid + ffn[...] + vec[6:7, :]).astype(BF)
    hat, scale = norm_stats(mid)
    grad = gn2[...]
    top = gs[...].astype(F32)
    total = top + norm_back(hat, scale, vec[2:3, :], grad)
    gm[...] = total
    low = total.astype(BF)
    ga[...] = low
    sums[...] = jnp.zeros(sums.shape, F32)
    sums[0:1, :] = jnp.sum(low.astype(F32), axis=0, keepdims=True)
    sums[1:2, :] = jnp.sum(grad * hat, axis=0, keepdims=True)
    sums[2:3, :] = jnp.sum(grad, axis=0, keepdims=True)
    sums[3:4, :] = jnp.sum(top, axis=0, keepdims=True)


def attend_back_body(assembled, *refs):
    order, ga, n1, *refs = refs
    if assembled:
        w, qkv, probs, ctx, gn_in, keep, away, brow, gn, gc, dqkv, full = refs
    else:
        own, oth, qkv, probs, ctx, gn_in, keep, away, brow, gn, gc, dqkv, full, w = refs
        put_back(order, own, oth, w)
    gc[...] = nt(ga[...], w[576:768, :]).astype(BF)
    for at, size, _ in PARTS:
        cut = slice(at, at + size)
        queries, keys, inner = (heads_of(qkv, cut, first) for first in (0, 192, 384))
        tops = heads_of(gc, cut, 0)
        low = [probs[h, cut, 0:size] for h in range(3)]
        p = [t.astype(F32) for t in low]
        gp = [nt(g, v) for g, v in zip(tops, inner)]
        ds = [
            (a * (b - jnp.sum(a * b, axis=-1, keepdims=True)) * 0.125).astype(BF)
            for a, b in zip(p, gp)
        ]
        dv = [tn(a, g).astype(BF) for a, g in zip(low, tops)]
        dq = [nn(a, k).astype(BF) for a, k in zip(ds, keys)]
        dk = [tn(a, q).astype(BF) for a, q in zip(ds, queries)]
        dqkv[cut, :] = jnp.concatenate(dq + dk + dv, axis=1)
    grads = dqkv[...]
    brow[...] = jnp.sum(grads.astype(F32), axis=0, keepdims=True)
    full[0:576, :] = tn(grads, n1[...]).astype(BF)
    full[576:768, :] = tn(ctx[...], ga[...]).astype(BF)
    for j in range(8):
        at = pl.multiple_of(order[j] * 96, 96)
        (keep, away)[j // 4][j % 4, :, :] = full[pl.ds(at, 96), :]
    gn[...] = gn_in[...] + nn(grads, w[0:576, :])


def last_body(order, xs, gm, gn1, vec, one, *refs):
    b1_rows, qkv_rows, rows_out, sums = refs[:4], refs[4:8], refs[8], refs[9]
    hat, scale = norm_stats(xs[...].astype(F32))
    grad = gn1[...]
    rows_out[...] = (gm[...] + norm_back(hat, scale, vec[0:1, :], grad)).astype(BF)
    sums[...] = jnp.zeros(sums.shape, F32)
    sums[0:1, :] = jnp.sum(grad * hat, axis=0, keepdims=True)
    sums[1:2, :] = jnp.sum(grad, axis=0, keepdims=True)
    sums[2:6, :] = one[0:4, :]
    for k in range(4):
        shard = order[8] ^ k
        sums[pl.ds(6 + shard, 1), :] = b1_rows[k][...]
        sums[pl.ds(10 + shard, 1), 0:576] = qkv_rows[k][...]


def hidden_final_body(order, own, oth, first, second, flat, flip, turned, sems):
    copies = []
    for j in range(8):
        at = pl.multiple_of(order[j] * 96, 96)
        part = (own, oth)[j // 4].at[j % 4]
        flat[96 * j : 96 * j + 96, :] = part[0:96, :].astype(F32)
        flip[pl.ds(at, 96), :] = part[96:192, :]
        copies.append(
            pltpu.make_async_copy(flat.at[pl.ds(96 * j, 96)], first.at[pl.ds(at, 96)], sems.at[j])
        )
        copies[-1].start()
    for i in range(6):
        cut = slice(128 * i, 128 * i + 128)
        turned[cut, :] = flip[:, cut].T.astype(F32)
        rows = pl.ds(128 * i, 128)
        copies.append(pltpu.make_async_copy(turned.at[rows], second.at[rows], sems.at[8 + i]))
        copies[-1].start()
    for copy in copies:
        copy.wait()


def attend_final_body(order, own, oth, qkv, out, full, sems):
    put_back(order, own, oth, full)
    copies = [
        pltpu.make_async_copy(full.at[pl.ds(192 * i, 192)], qkv.at[i] if i < 3 else out, sems.at[i])
        for i in range(4)
    ]
    for copy in copies:
        copy.start()
    for copy in copies:
        copy.wait()


GROUPS = {
    "ga": ((1,), (2, 3)),
    "gf": ((1,), (2,), (3,)),
    "f": ((0,), (1,), (2,), (3,)),
    "a": ((3,), (2,), (1,), (0,)),
}
JOINED = False
HALVES = ("f", "a")
COSTS = {
    "enda": 0.171,
    "attend2": 3.92,
    "hidden3": 8.0,
    "hidden0": 0.35,
    "back1": 0.8,
    "unout": 0.1,
    "unin": 8.0,
    "attend3": 8.0,
    "top": 0.7,
    "attend0": 0.07,
    "back2": 0.062,
    "copy": 0.1,
    "select": 4.0,
    "back0": 0.05,
    "hidden2": 0.25,
    "attend1": 8.0,
}
BEFORE = {
    "f0far": "hidden2",
    "f3far": "back2",
    "gf2own2": "enda",
    "gf1z": "last",
    "fzone": "last",
    "f0near": "back3",
    "a1near": "enda",
    "f0home": "enda",
    "xcore": "hidden0",
    "f3near": "unout",
    "gcore": "unin",
    "a3far": "back1",
    "a2far": "back1",
    "outcore": "back1",
    "f1near": "back2",
    "a3home": "back0",
    "out": "select",
    "f2far": "back2",
    "f2home": "unout",
    "gf1two": "last",
    "f1far": "turn",
    "ga1one": "top",
    "a2home": "back0",
    "ga23two": "attend0",
    "f2near": "back1",
    "ga2own2": "back2",
    "x": "attend1",
    "ga2two": "enda",
}
AFTER = {
    "ga3z": "hidden1",
    "hfone": "attend0",
    "g": "attend2",
    "f2home": "endf",
    "ga3two": "back0",
    "gf2one": "endf",
    "f1far": "back3",
    "haown": "top",
    "gf1own1": "unout",
    "gf3two": "back1",
    "a3far": "hidden0",
    "a0far": "unout",
    "f2far": "attend1",
    "ga1own1": "unout",
    "gf3one": "attend1",
    "ga1one": "attend3",
    "f3far": "unin",
    "ga2z": "attend0",
    "haone": "s3",
    "gf1one": "select",
    "a0near": "last",
    "azone": "s1",
    "aztwo": "s2",
    "hatwo": "s4",
}


class Plan:
    def __init__(self):
        self.makers, self.values, self.outputs = {}, {}, {}

    def payload(self, name, make, route):
        self.makers[name] = (make, route)

    def get(self, name):
        if name not in self.values:
            make, route = self.makers[name]
            value = make()
            late = AFTER.get(name)
            if late in self.outputs:
                value = after(value, self.outputs[late])
            elif late in self.makers:
                value = after(value, self.get(late)[0])
            self.values[name] = (value, value if route is None else send(value, route))
        return self.values[name]

    def arrived(self, name):
        return self.get(name)[1]

    def run(self, name, body, outs, args, us, scratch=(), hold=0, alias=None, out_far=False):
        gates = []
        for payload, late in BEFORE.items():
            if late == name:
                try:
                    gates.append(self.get(payload)[0])
                except KeyError:
                    pass
        args = list(args)
        if gates:
            args[hold] = after(args[hold], *gates)
        got = kernel(body, outs, args, us * COSTS.get(name, 1.0), scratch, (), alias, out_far)
        self.outputs[name] = got[-1]
        return got


def local(routes, *args):
    (
        inputs, crop_labels, norm1_gain, norm1_bias, qkv_weight, qv_bias, out_weight, out_bias,
        norm2_gain, norm2_bias, fc1_weight, fc1_bias, fc2_weight, fc2_bias, cotangent,
    ) = args
    dp, z = lax.axis_index("dp"), lax.axis_index("mp")
    c, x, y = dp & 1, (dp >> 1) & 1, (dp >> 2) & 1
    quarter = y * 2 + x
    mp = routes.mp
    eye = list(range(mp))
    f = lambda t: t.astype(F32)
    plan = Plan()

    def order_of(colour):
        near = jnp.where(colour == 0, 1, 2)
        far = 3 - near
        return [colour * 4 + (quarter ^ d) for d in (jnp.zeros_like(near), near, far, far + near)]

    order = jnp.stack(order_of(c) + order_of(1 - c) + [z]).astype(jnp.int32)

    start = (c * 4 + quarter) * 96
    heads_w = [jnp.swapaxes(qkv_weight, 1, 2).reshape(-1, D), out_weight]
    rows_a = lax.dynamic_slice_in_dim(jnp.concatenate(heads_w), start, 96)
    (piece_a,) = kernel(
        piece_body, [((112, D), BF)], [rows_a, fc1_bias[None], qv_bias], 0.3, room=8
    )
    wa0 = put_together(
        (D, D),
        [((slice(0, 576),), [(0, (Ellipsis,))]), ((slice(576, D),), [(1, (Ellipsis,))])],
        heads_w,
    )
    piece_f = put_together(
        (192, D),
        [((slice(96 * i, 96 * i + 96),), [(i, (Ellipsis,))]) for i in range(2)],
        [lax.dynamic_slice_in_dim(t, start, 96) for t in (fc1_weight, fc2_weight)],
    )

    owner = {}

    def legs(tag, slots, first, rows):
        def own(i):
            whole = slice(None)
            return put_together(
                (4, rows, D),
                [((slice(2 * j, 2 * j + 2),), [(j, (whole, i))]) for j in range(2)],
                plan.get(tag + "two"),
            )

        plan.payload(tag + "one", first, routes.first)
        plan.payload(
            tag + "two",
            lambda: put_together(
                (2, len(slots), rows, D),
                [((j,), [(j, (slice(None), slice(0, rows)))]) for j in range(2)],
                plan.get(tag + "one"),
            ),
            routes.second,
        )
        for i, k in enumerate(slots):
            owner[tag[:2], k] = f"{tag}own{k}"
            plan.payload(f"{tag}own{k}", lambda i=i: own(i), routes.core)

    for kind, piece, rows in (("ga", piece_a, 96), ("gf", piece_f, 192)):
        for k in eye[1:]:
            plan.payload(f"{kind}{k}z", lambda piece=piece: piece, routes.z[k])
        for slots in GROUPS[kind]:
            legs(
                kind + "".join(map(str, slots)), slots,
                lambda kind=kind, slots=slots: jnp.stack([plan.arrived(f"{kind}{k}z") for k in slots]),
                rows,
            )
    def rows_in_one():
        places = [((j,), [(j, (Ellipsis,))]) for j in range(2)]
        return put_together((2, HALF, D), places, [inputs, cotangent])

    plan.payload("x", rows_in_one if JOINED else lambda: inputs, routes.image)
    plan.payload("xcore", lambda: plan.arrived("x"), routes.core)
    plan.payload("g", lambda: cotangent, routes.image)
    plan.payload("gcore", lambda: plan.arrived("g"), routes.core)
    both = lambda name: plan.get(name)

    labels_here = crop_labels.reshape(-1, IMG_TOK)
    labels_there = send(labels_here, routes.core)
    smalls = [piece_a] + [plan.arrived(f"ga{k}z") for k in eye[1:]]

    labels = jnp.where((z & 1) == c, labels_here, labels_there)
    labels = lax.dynamic_index_in_dim(labels, z >> 1, axis=0, keepdims=False)
    row_here = targets(labels, c).reshape(2, HALF)
    row_there = targets(labels, 1 - c).reshape(2, HALF)
    row = lambda t, i: lax.dynamic_slice_in_dim(t, i, 1)
    row_own, row_oth, row_back = row(row_here, c), row(row_here, 1 - c), row(row_there, c)
    vec = jnp.stack(
        [f(t) for t in (norm1_gain, norm1_bias, norm2_gain, norm2_bias, fc2_bias, out_bias, fc2_bias, fc2_bias)]
    )

    low, high, turned = ((ROWS, D), BF), ((ROWS, D), F32), ((D, ROWS), BF)
    flip = [pltpu.VMEM((D, ROWS), BF)]
    whole = [pltpu.VMEM((D, D), BF)]
    block = lambda n: ((4, n, D), BF)

    xs, n1 = plan.run("select", select_body, [low, low], [*both("xcore"), row_own, row_oth, vec], 1.05)

    att = jnp.zeros((ROWS, D), F32)
    qkv, probs, ctx = [], [], []
    for k in eye:
        operands = [n1, wa0] if k == 0 else [order, n1, *both(owner["ga", k])]
        got = plan.run(
            f"attend{k}",
            lambda *refs, k=k: attend_body(k == 0, *refs),
            [((ROWS, 576), BF), ((3, ROWS, 256), BF), ((ROWS, 192), BF), high],
            operands + [smalls[k], att], 3.0, scratch=whole if k else (), hold=-2, alias={-1: 3},
        )
        qkv.append(got[0])
        probs.append(got[1])
        ctx.append(got[2])
        att = got[3]
    middle, n2, n2t = plan.run(
        "middle", middle_body, [high, low, turned], [order, xs, att, vec], 1.15, scratch=flip, hold=3
    )
    gs, gst = plan.run(
        "top", select_top_body, [low, turned], [order, *both("xcore" if JOINED else "gcore"), row_own, row_oth], 1.4,
        scratch=flip, hold=3,
    )

    parts = {}

    class Sum:
        def __init__(self, kind, slots):
            self.tag, self.kind, self.slots = kind + "".join(map(str, slots)), kind, slots
            plan.payload(self.tag + "far", lambda: self.gather(slice(2, 4)), routes.second)
            plan.payload(self.tag + "near", lambda: self.gather(1, ("far", (1,)), ), routes.first)
            for i, k in enumerate(slots):
                plan.payload(
                    f"{kind}{k}home",
                    lambda i=i: self.one(i),
                    routes.z[k] if k and kind not in HALVES else None,
                )

        def gather(self, part, *more):
            arrays = [t for k in self.slots for t in parts[self.kind, k]]
            arrays += [plan.arrived(self.tag + name) for name, _ in more]
            at = 2 * len(self.slots)
            rows = {"f": 192, "a": 96}[self.kind]
            pieces = [
                ((i,), [(2 * i, (part,)), (2 * i + 1, (part,))] + [(at + n, (i, *place)) for n, (_, place) in enumerate(more)])
                for i in range(len(self.slots))
            ]
            depth = (2,) if isinstance(part, slice) else ()
            return put_together((len(self.slots), *depth, rows, D), pieces, arrays)

        def one(self, i):
            keep, core = parts[self.kind, self.slots[i]]
            rows = {"f": 192, "a": 96}[self.kind]
            arrays = [keep, core, plan.arrived(self.tag + "far"), plan.arrived(self.tag + "near")]
            return put_together(
                (rows, D), [((Ellipsis,), [(0, (0,)), (1, (0,)), (2, (i, 0)), (3, (i,))])], arrays
            )

    for kind in ("f", "a"):
        for slots in GROUPS[kind]:
            Sum(kind, slots)
        if kind in HALVES:
            sent = lambda k, kind=kind: plan.get(f"{kind}{k}home")[0]
            plan.payload(kind + "zone", lambda sent=sent: jnp.stack([sent(1), sent(3)]), routes.z[1])
            plan.payload(
                kind + "ztwo",
                lambda sent=sent, kind=kind: (f(sent(2)) + f(plan.arrived(kind + "zone")[1])).astype(BF),
                routes.z[2],
            )

    def gather_up(tag):
        rows = {"f": 192, "a": 96}[tag]
        if tag in HALVES:
            arrays = [plan.get(f"{tag}0home")[0], plan.arrived(tag + "zone"), plan.arrived(tag + "ztwo")]
            places = [(0, (Ellipsis,)), (1, (0,)), (2, (Ellipsis,))]
        else:
            arrays = [plan.arrived(f"{tag}{k}home") for k in eye]
            places = [(k, (Ellipsis,)) for k in eye]
        total = put_together((1, rows, D), [((0,), places)], arrays)
        if not routes.group:
            return total
        total = f(total)
        for route in routes.group:
            total = total + f(send(total.astype(BF), route))
        return total.astype(BF)

    ffn = gn2 = jnp.zeros((ROWS, D), F32)
    b1_rows = []
    for k in eye:
        hold = [pltpu.VMEM((ROWS, D), BF)] * 2
        if k == 0:
            operands = [n2, gs, n2t, gst, fc1_weight, fc2_weight]
        else:
            operands = [order, n2, gs, n2t, gst, *both(owner["gf", k])]
            hold = hold + whole * 2
        keep, away, brow, ffn, gn2 = plan.run(
            f"hidden{k}",
            lambda *refs, k=k: hidden_body(k == 0, *refs),
            [block(192), block(192), ((1, D), F32), high, high],
            operands + [smalls[k], ffn, gn2], 4.0, scratch=hold, hold=-3, alias={-2: 3, -1: 4},
        )
        parts["f", k] = (keep, send(away, routes.core))
        b1_rows.append(brow)

    rows_out, gm, ga, sums_one = plan.run(
        "turn", turn_body, [low, high, low, ((8, D), F32)], [middle, ffn, gn2, gs, vec], 1.5, hold=4
    )
    plan.payload("outcore", lambda: rows_out, routes.core)

    def unselect(name, rows, there):
        return plan.run(
            name, unselect_body, [((HALF, D), BF)], [row_own, row_back, rows, there], 0.8, hold=2
        )[0]

    plan.payload("out", lambda: unselect("unout", *both("outcore")), routes.image)

    gn1 = jnp.zeros((ROWS, D), F32)
    qkv_rows = [None] * mp
    for k in reversed(eye):
        keep, away, brow, gn1 = plan.run(
            f"back{k}",
            lambda *refs, k=k: attend_back_body(k == 0, *refs),
            [block(96), block(96), ((1, 576), F32), high],
            [order, ga, n1, *([wa0] if k == 0 else both(owner["ga", k])), qkv[k], probs[k], ctx[k], gn1],
            5.0,
            scratch=[
                pltpu.VMEM((ROWS, 192), BF), pltpu.VMEM((ROWS, 576), BF), pltpu.VMEM((D, D), BF),
                *(whole if k else []),
            ],
            hold=0, alias={-1: 3},
        )
        parts["a", k] = (keep, send(away, routes.core))
        qkv_rows[k] = brow
    rows_in, sums = plan.run(
        "last", last_body, [low, ((16, D), F32)],
        [order, xs, gm, gn1, vec, sums_one, *b1_rows, *qkv_rows], 1.45, hold=4,
    )
    plan.payload("incore", lambda: rows_in, routes.core)
    plan.payload("in", lambda: unselect("unin", *both("incore")), routes.image)
    steps = [routes.core, routes.x, routes.y, routes.z[1], routes.z[2], *routes.group]
    plan.payload("s0", lambda: sums, steps[0])
    for i in range(1, len(steps) + 1):
        route = steps[i] if i < len(steps) else None
        plan.payload(f"s{i}", lambda i=i: sum(plan.get(f"s{i - 1}")), route)
    legs("hf", [""], lambda: gather_up("f"), 192)
    legs("ha", [""], lambda: gather_up("a"), 96)

    fc1_grad, fc2_grad = plan.run(
        "endf", hidden_final_body, [((D, D), F32)] * 2, [order, *both("hfown")], 3.7,
        scratch=[
            pltpu.VMEM((D, D), F32), pltpu.VMEM((D, D), BF), pltpu.VMEM((D, D), F32),
            pltpu.SemaphoreType.DMA((14,)),
        ],
        hold=1, out_far=True,
    )
    qkv_grad, out_grad = plan.run(
        "enda", attend_final_body, [((3, 192, D), F32), ((192, D), F32)], [order, *both("haown")], 2.2,
        scratch=[pltpu.VMEM((D, D), F32), pltpu.SemaphoreType.DMA((4,))], hold=1, out_far=True,
    )
    sums = plan.arrived(f"s{len(steps)}")
    rows_out, rows_in = plan.run(
        "copy", copy_body, [((HALF, D), BF)] * 2, [plan.arrived("out"), plan.arrived("in")], 1.2
    )
    qv_row = lax.dynamic_index_in_dim(sums, 10 + z, axis=0, keepdims=False)
    return (
        rows_out,
        rows_in,
        sums[0],
        sums[1],
        jnp.swapaxes(qkv_grad, 1, 2),
        jnp.stack([qv_row[:192], qv_row[384:576]]),
        out_grad,
        sums[2],
        sums[3],
        sums[4],
        fc1_grad,
        lax.dynamic_index_in_dim(sums, 6 + z, axis=0, keepdims=False),
        fc2_grad,
        sums[5],
    )


def solution(mesh):
    routes = Routes(mesh.shape["dp"], mesh.shape["mp"])
    placed = (
        P(ALL, None), P("dp"), P(), P(), P(None, None, "mp"), P(None, "mp"), P("mp", None), P(),
        P(), P(), P(None, "mp"), P("mp"), P("mp", None), P(), P(ALL, None),
    )
    given = (
        P(ALL, None), P(ALL, None), P(), P(), P(None, None, "mp"), P(None, "mp"), P("mp", None),
        P(), P(), P(), P(None, "mp"), P("mp"), P("mp", None), P(),
    )
    return jax.shard_map(
        lambda *args: local(routes, *args),
        mesh=mesh,
        in_specs=placed,
        out_specs=given,
        check_vma=False,
    )
```
